512 devices in a mesh: lat: 16 (over z_lo, y), row: 32 (over z_hi, x, core).
Axes of the slice: x: 4, y: 4, z: 16 (z_hi: 4, z_lo: 4; z = z_hi * 4 + z_lo), core: 2. Of those that a mesh axis runs over, the one named last changes fastest.
Arguments:
- g_wannier: bfloat16 [96, 300, 128, 256], P('lat', None, 'row'), may hold values from -0.8984375 to 0.8984375
- lattice: int32 [96, 3], P('lat'), may hold values from -6 to 6
- degeneracy: int32 [96], P('lat'), may hold values from 1 to 5
- qgrid: int32 [8, 3], replicated, may hold values from 0 to 39
- phonon_vectors: bfloat16 [8, 288, 600], P(None, 'lat'), may hold values from -0.25 to 0.25
- wannier_k: bfloat16 [128, 256], replicated, may hold values from -0.375 to 0.375
- wannier_kq: bfloat16 [8, 128, 256], replicated, may hold values from -0.375 to 0.375
Outputs:
- coupling: float32 [288, 8, 128, 256], P('lat', None, 'row')
The draws below stay inside these ranges and needn't reach their ends.
All inputs are finite; a program needn't handle non-finite values.
Results may differ from the reference program's by a relative error of at most 0.024.
Values may be sent and summed in bfloat16 or wider, within the bound.
A program may use at most 64 MiB of HBM per device.

```python
import math
import jax
import jax.numpy as jnp
from jax import lax

NW = 128
MODES = 300
NU = 288
R_DEV = 6
Q_PTS = 8
FINE = 40
RVECS = 96
N_LAT = 16


def set_ends(result, key, least, top_value):
    longest = result.shape.index(max(result.shape))
    spots = []
    for shift in (0, 1):
        where = [jax.random.randint(jax.random.fold_in(key, axis), (), 0, length) for axis, length in enumerate(result.shape)]
        where[longest] = (where[longest] + shift) % result.shape[longest]
        spots.append(tuple(where))
    return result.at[spots[0]].set(least).at[spots[1]].set(top_value)


def levels(stream_key, dims, cuts, least, largest):
    loudness = 1.0
    for dim, shards_of in cuts:
        steps = jax.random.uniform(jax.random.fold_in(jax.random.fold_in(stream_key, 6), dim), (shards_of,), jnp.float32, least / len(cuts), largest / len(cuts))
        loudness = loudness * jnp.repeat(jnp.exp(steps), dims[dim] // shards_of).reshape((-1,) + (1,) * (len(dims) - 1 - dim))
    return loudness


def normal_values(key, extent, scale, bound, cuts=(), held_as=jnp.bfloat16):
    gain = levels(key, extent, cuts, -0.22, 0.18) if cuts else 1.0
    drawn = jax.random.normal(key, extent, jnp.float32) * scale * gain
    return jnp.minimum(jnp.maximum(drawn, -bound), bound).astype(held_as)


def setup_inputs(seed: int = 0) -> dict:
    key_list = jax.random.split(jax.random.key(seed), 8)
    return {
        "g_wannier": normal_values(key_list[0], (RVECS, MODES, NW, 2 * NW), 0.15, 0.8984375, ((0, 16), (2, 32))),
        "lattice": set_ends(jax.random.randint(key_list[1], (RVECS, 3), -6, 7), jax.random.fold_in(key_list[1], 1), -6, 6).astype(jnp.int32),
        "degeneracy": set_ends(jax.random.randint(key_list[2], (RVECS,), 1, 6), jax.random.fold_in(key_list[2], 1), 1, 5).astype(jnp.int32),
        "qgrid": set_ends(jax.random.randint(key_list[3], (Q_PTS, 3), 0, FINE), jax.random.fold_in(key_list[3], 1), 0, FINE - 1).astype(jnp.int32),
        "phonon_vectors": normal_values(key_list[4], (Q_PTS, NU, 2 * MODES), (2 * MODES) ** -0.5, 0.25, ((1, 16),)),
        "wannier_k": normal_values(key_list[5], (NW, 2 * NW), (2 * NW) ** -0.5, 0.375),
        "wannier_kq": normal_values(key_list[6], (Q_PTS, NW, 2 * NW), (2 * NW) ** -0.5, 0.375),
    }


def phases(qgrid, lattice, degeneracy):
    product = jnp.sum(qgrid[:, None, :] * lattice[None, :, :], axis=-1) % FINE
    angle = (2.0 * math.pi / FINE) * product.astype(jnp.float32)
    weight = 1.0 / degeneracy.astype(jnp.float32)
    return jnp.cos(angle) * weight[None, :], jnp.sin(angle) * weight[None, :]


def reference(g_wannier, lattice, degeneracy, qgrid, phonon_vectors, wannier_k, wannier_kq):
    cosines, sines = phases(qgrid, lattice, degeneracy)
    er = phonon_vectors[:, :, :MODES]
    ei = phonon_vectors[:, :, MODES:]
    emat = jnp.stack([jnp.concatenate([er, -ei], -1), jnp.concatenate([ei, er], -1)], axis=2).astype(jnp.float32)
    grouped = g_wannier.reshape(N_LAT, R_DEV, MODES * NW * 2 * NW)
    cos_grp = jnp.transpose(cosines.reshape(Q_PTS, N_LAT, R_DEV), (1, 0, 2))
    sin_grp = jnp.transpose(sines.reshape(Q_PTS, N_LAT, R_DEV), (1, 0, 2))

    def one_group(total, item):
        block, cos_part, sin_part = item
        block32 = block.astype(jnp.float32)
        first = jnp.dot(cos_part, block32, precision=lax.Precision.HIGHEST).reshape(Q_PTS, MODES, NW, 2, NW)
        second = jnp.dot(sin_part, block32, precision=lax.Precision.HIGHEST).reshape(Q_PTS, MODES, NW, 2, NW)
        real_part = first[:, :, :, 0] - second[:, :, :, 1]
        imag_part = first[:, :, :, 1] + second[:, :, :, 0]
        stacked = jnp.concatenate([real_part, imag_part], axis=1).reshape(Q_PTS, 2 * MODES, NW * NW)
        stacked = stacked.astype(jnp.bfloat16).astype(jnp.float32)
        term = jnp.einsum("qvck,qkx->vqcx", emat, stacked)
        rounded = lax.optimization_barrier(term.astype(jnp.bfloat16))
        return total + rounded.astype(jnp.float32), None

    start = jnp.zeros((NU, Q_PTS, 2, NW * NW), jnp.float32)
    total, _ = lax.scan(one_group, start, (grouped, cos_grp, sin_grp))
    summed = total.astype(jnp.bfloat16).astype(jnp.float32).reshape(NU, Q_PTS, 2, NW, NW)
    uk_imag = wannier_k[:, NW:]
    uk_real = wannier_k[:, :NW]
    right_mat = jnp.concatenate([wannier_k, jnp.concatenate([-uk_imag, uk_real], 1)], 0)
    right_mat = right_mat.astype(jnp.float32).reshape(2, NW, 2 * NW)
    rotated = jnp.einsum("vqcmn,cnx->vqmx", summed, right_mat).astype(jnp.bfloat16)
    rotated = rotated.astype(jnp.float32).reshape(NU, Q_PTS, NW, 2, NW)
    ur = wannier_kq[:, :, :NW]
    ui = wannier_kq[:, :, NW:]
    left_mat = jnp.stack([jnp.concatenate([ur, -ui], -1), jnp.concatenate([ui, ur], -1)], axis=1).astype(jnp.float32)
    return jnp.einsum("vqmcn,qcmx->vqnx", rotated, left_mat)
```

```python
import functools
import math

import jax
import jax.numpy as jnp
from jax import lax
from jax.experimental import pallas as pl
from jax.experimental.pallas import tpu as pltpu
from jax.sharding import PartitionSpec as P

FINE = 40
NY = 4
NZ = 4
MESH = pl.DeviceIdType.MESH
F32 = jnp.float32
BF16 = jnp.bfloat16


def dot(a, b, contract=((1,), (0,))):
    return lax.dot_general(a, b, (contract, ((), ())), preferred_element_type=F32)


def times_i(x):
    half = x.shape[-1] // 2
    return jnp.concatenate([-x[:, half:], x[:, :half]], axis=1)


def kernel(rows, g_ref, a_ref, e_ref, rt_ref, l_ref, out_ref,
           part, yfar, ynear, e1, e2, e3, ef, eb, spart, zin, sfull, kt, kr, zf, ob, osend,
           yf_s, yf_r, yn_s, yn_r, e_s, e_r, z_s, z_r, row_s, row_r, o_s, o_r):
    n_lat, n_row = NY * NZ, rows
    lat = lax.axis_index("lat")
    row = lax.axis_index("row")
    y = lax.rem(lat, NY)
    z = lax.div(lat, NY)
    core = lax.rem(row, 2)
    n_r = g_ref.shape[1]
    modes = g_ref.shape[2]
    nv = e_ref.shape[1]
    vz = NY * nv

    def ypeer(d):
        return z * NY + lax.rem(y + d, NY)

    def zpeer(d):
        return lax.rem(z + d, NZ) * NY + y

    def remote(src, dst, ss, rs, **dev):
        return pltpu.make_async_remote_copy(
            src_ref=src, dst_ref=dst, send_sem=ss, recv_sem=rs, device_id=dev, device_id_type=MESH)

    barrier = pltpu.get_barrier_semaphore()
    for d in range(1, NY):
        pl.semaphore_signal(barrier, inc=1, device_id={"lat": ypeer(d)}, device_id_type=MESH)
    for d in range(1, NZ):
        pl.semaphore_signal(barrier, inc=1, device_id={"lat": zpeer(d)}, device_id_type=MESH)

    @pl.loop(1, n_row)
    def _(p):
        pl.semaphore_signal(barrier, inc=1, device_id={"row": lax.rem(row + p, n_row)}, device_id_type=MESH)

    pl.semaphore_wait(barrier, NY + NZ - 2 + n_row - 1)

    def e1_copy(d):
        yy = lax.rem(y + d, NY)
        return remote(e_ref.at[2 * yy + core], e1.at[y], e_s.at[d], e_r.at[y], lat=ypeer(d))

    def e1_in(d):
        yy = lax.rem(y + d, NY)
        return remote(e_ref.at[2 * yy + core], e1.at[yy], e_s.at[d], e_r.at[yy], lat=ypeer(d))

    def e2_copy(d):
        return remote(e1, e2.at[z], e_s.at[NY + d], e_r.at[NY + z], lat=zpeer(d))

    def e2_in(d):
        zz = lax.rem(z + d, NZ)
        return remote(e1, e2.at[zz], e_s.at[NY + d], e_r.at[NY + zz], lat=zpeer(d))

    def e3_copy():
        return remote(e2, e3, e_s.at[NY + NZ], e_r.at[NY + NZ], row=row + 1 - 2 * core)

    for d in range(1, NY):
        e1_copy(d).start()
    e1[y] = e_ref[2 * y + core]

    def phase_sums(m):
        for i in range(modes // 16):
            blocks = [g_ref[m, r, 16 * i:16 * i + 16, :] for r in range(n_r)]
            stack = jnp.concatenate(blocks + [times_i(b) for b in blocks], axis=0)
            res = dot(a_ref[...], stack).astype(BF16)
            for q in range(8):
                part[q, m, 16 * i:16 * i + 16, :] = res[16 * q:16 * q + 16, :]

    right, left = ypeer(1), ypeer(3)
    qa = 2 * lax.rem(y + 1, NY)
    qb = 2 * lax.rem(y + 2, NY)
    qc = 2 * lax.rem(y + 3, NY)

    def far(s, way):
        h, k = divmod(s, 2)
        return remote(part.at[qb + k, h + 2 * way], yfar.at[s, way], yf_s.at[s, way], yf_r.at[s, way],
                      lat=(right, left)[way])

    def near(s, way, half):
        h, k = divmod(s, 2)
        q = (qa, qc)[way] + k
        return remote(part.at[q, h + 2 * half], ynear.at[s, way, half], yn_s.at[s, way, half],
                      yn_r.at[s, way, half], lat=(right, left)[way])

    def start_far(s):
        for way in (0, 1):
            far(s, way).start()

    def start_own(s):
        for way in (0, 1):
            near(s, way, 1 - way).start()

    def start_sums(s):
        h, k = divmod(s, 2)
        for way in (0, 1):
            far(s, way).wait_recv()
            q = (qa, qc)[way] + k
            m = h + 2 * way
            part[q, m] = (part[q, m].astype(F32) + yfar[s, way].astype(F32)).astype(BF16)
            near(s, way, way).start()

    def branch(s):
        h, k = divmod(s, 2)
        for way in (0, 1):
            for half in (0, 1):
                near(s, way, half).wait_recv()
        res = []
        for half in (0, 1):
            total = (part[2 * y + k, h + 2 * half].astype(F32) + ynear[s, 0, half].astype(F32)
                     + ynear[s, 1, half].astype(F32)).astype(BF16)
            both = jnp.concatenate([total, times_i(total)], axis=0)
            res.append(dot(eb[k], both))
        for zz in range(NZ):
            spart[s, zz] = jnp.concatenate([r[vz * zz:vz * zz + vz] for r in res], axis=0).astype(BF16)
        for d in range(1, NZ):
            z_copy(s, d).start()

    def z_copy(s, d):
        return remote(spart.at[s, lax.rem(z + d, NZ)], zin.at[s, z], z_s.at[s, d], z_r.at[s, z], lat=zpeer(d))

    def z_in(s, d):
        zz = lax.rem(z + d, NZ)
        return remote(spart.at[s, zz], zin.at[s, zz], z_s.at[s, d], z_r.at[s, zz], lat=zpeer(d))

    def z_sum(s):
        h, k = divmod(s, 2)
        total = spart[s, z].astype(F32)
        for d in range(1, NZ):
            z_in(s, d).wait_recv()
            total = total + zin[s, lax.rem(z + d, NZ)].astype(F32)
        size = 2 * vz
        sfull[h, size * k:size * k + size, :] = total.astype(BF16)

    def row_copy(h, p):
        to = lax.rem(row + p, n_row)
        return remote(kt.at[h, to], kr.at[h, row], row_s.at[h, p], row_r.at[h, row], row=to)

    def row_in(h, p):
        other = lax.rem(row + p, n_row)
        return remote(kt.at[h, other], kr.at[h, other], row_s.at[h, p], row_r.at[h, other], row=other)

    def right_rotate(h):
        res = dot(rt_ref[...], sfull[h], ((1,), (1,)))
        kt[h] = res.reshape(kt.shape[1:]).astype(BF16)

        @pl.loop(1, n_row)
        def _(p):
            row_copy(h, p).start()

        kr[h, row] = kt[h, row]

    def left_rotate(h):
        @pl.loop(1, n_row)
        def _(p):
            row_in(h, p).wait_recv()

        tiles = zf.shape[0]
        got = kr[h].astype(F32).reshape(zf.shape[1], 128 * tiles)
        for t in range(tiles):
            zf[t] = got[:, 128 * t:128 * t + 128]
        for n in range(4):
            w = jnp.concatenate([zf[t, pl.ds(n, 2 * n_row, stride=4), :].T for t in range(tiles)], axis=0)
            for k in (0, 1):
                acc = None
                for half in (0, 1):
                    at = 2 * vz * k + vz * half
                    term = dot(w[at:at + vz].astype(BF16), l_ref[2 * y + k, h + 2 * half])
                    acc = term if acc is None else acc + term
                for t in range(2):
                    here = acc[:, 128 * t:128 * t + 128]
                    if h:
                        here = here + ob[k, t, pl.ds(n, vz, stride=4), :]
                    ob[k, t, pl.ds(n, vz, stride=4), :] = here

    sfull[:, 4 * vz:, :] = jnp.zeros((2, sfull.shape[1] - 4 * vz, sfull.shape[2]), BF16)
    phase_sums(0)
    phase_sums(2)
    start_far(0)
    start_own(0)
    start_far(1)
    for d in range(1, NY):
        e1_in(d).wait_recv()
    for d in range(1, NZ):
        e2_copy(d).start()
    e2[z] = e1[...]
    phase_sums(1)
    phase_sums(3)
    start_sums(0)
    start_own(1)
    start_far(2)
    for d in range(1, NZ):
        e2_in(d).wait_recv()
    e3_copy().start()
    for l in range(n_lat):
        ef[nv * l:nv * l + nv, :] = e2[l // NY, l % NY].astype(F32)
    eb[core] = ef[...].astype(BF16)
    e3_copy().wait_recv()
    for l in range(n_lat):
        ef[nv * l:nv * l + nv, :] = e3[l // NY, l % NY].astype(F32)
    eb[1 - core] = ef[...].astype(BF16)
    start_sums(1)
    start_own(2)
    start_far(3)
    branch(0)
    start_sums(2)
    start_own(3)
    z_sum(0)
    branch(1)
    start_sums(3)
    z_sum(1)
    right_rotate(0)
    branch(2)
    z_sum(2)
    branch(3)
    left_rotate(0)
    z_sum(3)
    right_rotate(1)
    left_rotate(1)

    def o_copy(d):
        return remote(osend.at[lax.rem(y + d, NY)], out_ref.at[y], o_s.at[d], o_r.at[y], lat=ypeer(d))

    def o_in(d):
        yy = lax.rem(y + d, NY)
        return remote(osend.at[yy], out_ref.at[yy], o_s.at[d], o_r.at[yy], lat=ypeer(d))

    size = 4 * nv
    for yy in range(NY):
        osend[yy] = jnp.concatenate(
            [jnp.concatenate([ob[k, t, size * yy:size * yy + size, :] for t in range(2)], axis=1) for k in (0, 1)],
            axis=0).astype(BF16)
    for d in range(1, NY):
        o_copy(d).start()
    out_ref[y] = osend[y]

    for d in range(1, NY):
        e1_copy(d).wait_send()
    for d in range(1, NZ):
        e2_copy(d).wait_send()
    e3_copy().wait_send()
    for s in range(4):
        for way in (0, 1):
            far(s, way).wait_send()
            for half in (0, 1):
                near(s, way, half).wait_send()
        for d in range(1, NZ):
            z_copy(s, d).wait_send()
    for h in (0, 1):
        @pl.loop(1, n_row)
        def _(p):
            row_copy(h, p).wait_send()
    for d in range(1, NY):
        o_in(d).wait_recv()
        o_copy(d).wait_send()


def phases(qgrid, lattice, degeneracy):
    product = jnp.sum(qgrid[:, None, :] * lattice[None, :, :], axis=-1) % FINE
    angle = 2.0 * math.pi / FINE * product.astype(F32)
    weight = 1.0 / degeneracy.astype(F32)
    return jnp.cos(angle) * weight[None, :], jnp.sin(angle) * weight[None, :]


def per_device(n_row, g_wannier, lattice, degeneracy, qgrid, phonon_vectors, wannier_k, wannier_kq):
    n_r, modes, rows_m, wide = g_wannier.shape
    width = wide // 2
    points, nv, _ = phonon_vectors.shape
    full = -(-modes // 16) * 16
    vz = NY * nv
    lanes = -(-4 * vz // 128) * 128

    cosines, sines = phases(qgrid, lattice, degeneracy)
    phase = jnp.concatenate([cosines, sines], axis=1).astype(BF16)
    a = (phase[:, None, :, None] * jnp.eye(16, dtype=BF16)[None, :, None, :]).reshape(points * 16, 2 * n_r * 16)
    g = jnp.pad(jnp.transpose(g_wannier, (2, 0, 1, 3)), ((0, 0), (0, 0), (0, full - modes), (0, 0)))
    e = jnp.pad(phonon_vectors.reshape(points, nv, 2, modes), ((0, 0), (0, 0), (0, 0), (0, full - modes)))
    e = e.reshape(points, nv, 2 * full)
    uk_real, uk_imag = wannier_k[:, :width], wannier_k[:, width:]
    right = jnp.concatenate([wannier_k, jnp.concatenate([-uk_imag, uk_real], 1)], 0)
    rt = right.T.reshape(2, n_row, width // n_row, wide).transpose(1, 0, 2, 3).reshape(wide, wide)
    ur, ui = wannier_kq[:, :, :width], wannier_kq[:, :, width:]
    left = jnp.stack([jnp.concatenate([ur, -ui], -1), jnp.concatenate([ui, ur], -1)], axis=1)
    left = left.reshape(points, 2, n_row, rows_m, wide).transpose(0, 3, 2, 1, 4).reshape(points, rows_m, 2 * n_row, wide)

    dma = pltpu.SemaphoreType.DMA
    vmem = pl.BlockSpec(memory_space=pltpu.VMEM)
    out = pl.pallas_call(
        functools.partial(kernel, n_row),
        out_shape=jax.ShapeDtypeStruct((NY, 8 * nv, wide), BF16),
        in_specs=[vmem] * 5,
        out_specs=vmem,
        scratch_shapes=[
            pltpu.VMEM((points, rows_m, full, wide), BF16),
            pltpu.VMEM((4, 2, full, wide), BF16),
            pltpu.VMEM((4, 2, 2, full, wide), BF16),
            pltpu.VMEM((NY, nv, 2 * full), BF16),
            pltpu.VMEM((NZ, NY, nv, 2 * full), BF16),
            pltpu.VMEM((NZ, NY, nv, 2 * full), BF16),
            pltpu.VMEM((NZ * vz, 2 * full), F32),
            pltpu.VMEM((2, NZ * vz, 2 * full), BF16),
            pltpu.VMEM((4, NZ, 2 * vz, wide), BF16),
            pltpu.VMEM((4, NZ, 2 * vz, wide), BF16),
            pltpu.VMEM((2, lanes, wide), BF16),
            pltpu.VMEM((2, n_row, wide // n_row, lanes), BF16),
            pltpu.VMEM((2, n_row, wide // n_row, lanes), BF16),
            pltpu.VMEM((lanes // 128, wide, 128), F32),
            pltpu.VMEM((2, 2, 4 * vz, width), F32),
            pltpu.VMEM((NY, 8 * nv, wide), BF16),
            dma((4, 2)), dma((4, 2)),
            dma((4, 2, 2)), dma((4, 2, 2)),
            dma((NY + NZ + 1,)), dma((NY + NZ + 1,)),
            dma((4, NZ)), dma((4, NZ)),
            dma((2, n_row)), dma((2, n_row)),
            dma((NY,)), dma((NY,)),
        ],
        compiler_params=pltpu.CompilerParams(
            collective_id=0, has_side_effects=True, vmem_limit_bytes=48 * 1024 * 1024),
        name="interpolate",
    )(g, a, e, rt, left)
    out = out.reshape(NY, 2, nv, 4, wide).transpose(2, 0, 1, 3, 4)
    return out.reshape(nv, points, 4, wide).astype(F32)


def solution(mesh):
    in_specs = (
        P("lat", None, "row", None),
        P("lat", None),
        P("lat"),
        P(),
        P(None, "lat", None),
        P(),
        P(),
    )
    out_specs = P("lat", None, "row", None)
    return jax.shard_map(
        functools.partial(per_device, mesh.shape["row"]),
        mesh=mesh, in_specs=in_specs, out_specs=out_specs, check_vma=False)
```

```python
import functools
import math

import jax
import jax.numpy as jnp
from jax import lax
from jax.experimental import pallas as pl
from jax.experimental.pallas import tpu as pltpu
from jax.sharding import PartitionSpec as P

FINE = 40
NY = 4
NZ = 4
MESH = pl.DeviceIdType.MESH
F32 = jnp.float32
BF16 = jnp.bfloat16


def dot(a, b, contract=((1,), (0,))):
    return lax.dot_general(a, b, (contract, ((), ())), preferred_element_type=F32)


def times_i(x):
    half = x.shape[-1] // 2
    return jnp.concatenate([-x[:, half:], x[:, :half]], axis=1)


def iota(shape, dim):
    return lax.broadcasted_iota(jnp.int32, shape, dim)


def one_hot(condition):
    return jnp.where(condition, 1.0, 0.0).astype(BF16)


UNITS = 8
COLUMN = (0, 72, 144, 216, 288, 360, 432, 512)
WINDOWS = ((0, 256), (256, 384), (384, 512), (512, 640))


def kernel(rows, g_ref, tail_ref, ph_ref, e_ref, wk_ref, wkq_ref, out_ref,
           part, yfar, ynear, e1, e2, e3, ef, eb, spart, zin_a, zmid, zin_b, sfull, rt, lf, lb,
           kt0, kt1, kt2, kt3, kr0, kr1, kr2, kr3, zf, ob, osend,
           yf_s, yf_r, yn_s, yn_r, e_s, e_r, za_s, za_r, zb_s, zb_r, row_s, row_r, o_s, o_r):
    n_row = rows
    kt, kr = (kt0, kt1, kt2, kt3), (kr0, kr1, kr2, kr3)
    lat = lax.axis_index("lat")
    row = lax.axis_index("row")
    y = lax.rem(lat, NY)
    z = lax.div(lat, NY)
    z_par, z_half = lax.rem(z, 2), lax.div(z, 2)
    core = lax.rem(row, 2)
    n_r, modes = g_ref.shape[1], g_ref.shape[2]
    full = part.shape[2]
    nv = e_ref.shape[1]
    vz = NY * nv

    def ypeer(d):
        return z * NY + lax.rem(y + d, NY)

    def zpeer(d):
        return lax.rem(z + d, NZ) * NY + y

    def remote(src, dst, ss, rs, **dev):
        return pltpu.make_async_remote_copy(
            src_ref=src, dst_ref=dst, send_sem=ss, recv_sem=rs, device_id=dev, device_id_type=MESH)

    barrier = pltpu.get_barrier_semaphore()
    for d in range(1, NY):
        pl.semaphore_signal(barrier, inc=1, device_id={"lat": ypeer(d)}, device_id_type=MESH)
    for d in range(1, NZ):
        pl.semaphore_signal(barrier, inc=1, device_id={"lat": zpeer(d)}, device_id_type=MESH)

    @pl.loop(1, n_row)
    def _(p):
        pl.semaphore_signal(barrier, inc=1, device_id={"row": lax.rem(row + p, n_row)}, device_id_type=MESH)

    spread_rows = one_hot((iota((128, 16), 0) >> 4) == iota((128, 16), 1))
    spread_cols = one_hot(iota((128, 32 * n_r), 0) == (iota((128, 32 * n_r), 1) >> 4))
    same = (iota((128, 32 * n_r), 0) & 15) == (iota((128, 32 * n_r), 1) & 15)
    a = jnp.where(same, dot(dot(spread_rows, ph_ref[...]).astype(BF16), spread_cols), 0.0).astype(BF16)

    def phase_sums(m):
        for i in range(full // 16):
            if 16 * i + 16 <= modes:
                blocks = [g_ref[m, r, 16 * i:16 * i + 16, :] for r in range(n_r)]
            else:
                blocks = [tail_ref[m, r] for r in range(n_r)]
            stack = jnp.concatenate(blocks + [times_i(b) for b in blocks], axis=0)
            res = dot(a, stack).astype(BF16)
            for q in range(8):
                part[q, m, 16 * i:16 * i + 16, :] = res[16 * q:16 * q + 16, :]

    def e1_copy(d):
        yy = lax.rem(y + d, NY)
        return remote(e_ref.at[2 * yy + core], e1.at[y], e_s.at[d], e_r.at[y], lat=ypeer(d))

    def e1_in(d):
        yy = lax.rem(y + d, NY)
        return remote(e_ref.at[2 * yy + core], e1.at[yy], e_s.at[d], e_r.at[yy], lat=ypeer(d))

    def e2_copy(d):
        return remote(e2.at[z], e2.at[z], e_s.at[NY + d], e_r.at[NY + z], lat=zpeer(d))

    def e2_in(d):
        zz = lax.rem(z + d, NZ)
        return remote(e2.at[zz], e2.at[zz], e_s.at[NY + d], e_r.at[NY + zz], lat=zpeer(d))

    def e3_copy():
        return remote(e2, e3, e_s.at[NY + NZ], e_r.at[NY + NZ], row=row + 1 - 2 * core)

    def eigenvectors(source, k):
        whole = jnp.concatenate([source[zz].astype(F32) for zz in range(NZ)], axis=0).astype(BF16)
        at = iota((2 * modes, 2 * full), 0)
        to = iota((2 * modes, 2 * full), 1)
        spread = one_hot(jnp.where(at < modes, at, at + full - modes) == to)
        eb[k] = dot(whole, spread).astype(BF16)

    right, left = ypeer(1), ypeer(3)
    qa = 2 * lax.rem(y + 1, NY)
    qb = 2 * lax.rem(y + 2, NY)
    qc = 2 * lax.rem(y + 3, NY)

    def ways(u):
        cut = (full // 2 + 15) // 16 * 16
        cut = cut if u % 2 == 0 else full - cut
        return pl.ds(0, cut), pl.ds(cut, full - cut)

    def far(u, way):
        m, k = divmod(u, 2)
        here = ways(u)[way]
        return remote(part.at[qb + k, m, here], yfar.at[u, here], yf_s.at[u, way], yf_r.at[u, way],
                      lat=(right, left)[way])

    def near(u, way, half):
        m, k = divmod(u, 2)
        here = ways(u)[half]
        q = (qa, qc)[way] + k
        return remote(part.at[q, m, here], ynear.at[u, way, here], yn_s.at[u, way, half],
                      yn_r.at[u, way, half], lat=(right, left)[way])

    def start_far(u):
        for way in (0, 1):
            far(u, way).start()

    def start_own(u):
        for way in (0, 1):
            near(u, way, 1 - way).start()

    def start_sums(u):
        m, k = divmod(u, 2)
        for way in (0, 1):
            far(u, way).wait_recv()
            q = (qa, qc)[way] + k
            here = ways(u)[way]
            part[q, m, here, :] = (part[q, m, here, :].astype(F32) + yfar[u, here, :].astype(F32)).astype(BF16)
            near(u, way, way).start()

    def z_copy_a(u):
        return remote(spart.at[u, 1 - z_par], zin_a.at[u], za_s.at[u], za_r.at[u],
                      lat=(z + 1 - 2 * z_par) * NY + y)

    def z_copy_b(u):
        return remote(zmid.at[u], zin_b.at[u], zb_s.at[u], zb_r.at[u], lat=zpeer(2))

    def branch(u):
        m, k = divmod(u, 2)
        for way in (0, 1):
            for half in (0, 1):
                near(u, way, half).wait_recv()
        total = (part[2 * y + k, m].astype(F32) + ynear[u, 0].astype(F32) + ynear[u, 1].astype(F32)).astype(BF16)
        res = dot(eb[k], jnp.concatenate([total, times_i(total)], axis=0))
        for zz in range(NZ):
            spart[u, zz % 2, zz // 2] = res[vz * zz:vz * zz + vz].astype(BF16)
        z_copy_a(u).start()

    def z_middle(u):
        z_copy_a(u).wait_recv()
        other = 1 - z_half
        zmid[u] = (spart[u, z_par, other].astype(F32) + zin_a[u, other].astype(F32)).astype(BF16)
        z_copy_b(u).start()

    def z_end(u):
        own = spart[u, z_par, z_half].astype(F32) + zin_a[u, z_half].astype(F32)
        z_copy_b(u).wait_recv()
        sfull[COLUMN[u]:COLUMN[u] + vz, :] = own + zin_b[u].astype(F32)

    def row_copy(w, p):
        to = lax.rem(row + p, n_row)
        return remote(kt[w].at[to], kr[w].at[row], row_s.at[w, p], row_r.at[w, row], row=to)

    def row_in(w, p):
        other = lax.rem(row + p, n_row)
        return remote(kt[w].at[other], kr[w].at[other], row_s.at[w, p], row_r.at[w, other], row=other)

    def right_rotate(w):
        lo, hi = WINDOWS[w]
        res = dot(rt[...], sfull[lo:hi, :].astype(BF16), ((1,), (1,)))
        kt[w][...] = res.reshape(kt[w].shape).astype(BF16)

        @pl.loop(1, n_row)
        def _(p):
            row_copy(w, p).start()

        kr[w][row] = kt[w][row]

    def row_wait(w):
        @pl.loop(1, n_row)
        def _(p):
            row_in(w, p).wait_recv()

        lo, hi = WINDOWS[w]
        got = kr[w][...].astype(F32).reshape(8 * n_row, hi - lo)
        for t in range((hi - lo) // 128):
            zf[lo // 128 + t] = got[:, 128 * t:128 * t + 128]

    def left_rotate(units, first):
        lo = COLUMN[units[0]] // 128
        hi = -(-(COLUMN[units[-1]] + vz) // 128)
        for n in range(4):
            w = jnp.concatenate(
                [jnp.concatenate([zf[t, pl.ds(n + 4 * c, n_row, stride=8), :] for c in (0, 1)], axis=0).T
                 for t in range(lo, hi)], axis=0)
            for k in (0, 1):
                acc = None
                for u in units:
                    if u % 2 == k:
                        at = COLUMN[u] - 128 * lo
                        term = dot(w[at:at + vz].astype(BF16), lb[u])
                        acc = term if acc is None else acc + term
                if acc is None:
                    continue
                for t in range(2):
                    here = acc[:, 128 * t:128 * t + 128]
                    if not first:
                        here = here + ob[k, t, pl.ds(n, vz, stride=4), :]
                    ob[k, t, pl.ds(n, vz, stride=4), :] = here

    def rotations():
        r, j = iota((256, 256), 0), iota((256, 256), 1)
        perm = one_hot(j == ((r >> 2) & 1) * 128 + (r >> 3) * 4 + (r & 3))
        both = jnp.concatenate([wk_ref[...], times_i(wk_ref[...])], axis=0)
        rt[...] = dot(perm, both, ((1,), (1,))).astype(BF16)
        for k in (0, 1):
            for t in (0, 1):
                lf[k, t] = wkq_ref[2 * y + k, :, 128 * t:128 * t + 128].astype(F32)
        for u in range(UNITS):
            m, k = divmod(u, 2)
            ur = lf[k, 0, pl.ds(m, n_row, stride=4), :]
            ui = lf[k, 1, pl.ds(m, n_row, stride=4), :]
            lb[u] = jnp.concatenate([jnp.concatenate([ur, -ui], axis=1), jnp.concatenate([ui, ur], axis=1)],
                                    axis=0).astype(BF16)
        sfull[COLUMN[6] + vz:COLUMN[7], :] = jnp.zeros((COLUMN[7] - COLUMN[6] - vz, 256), F32)
        sfull[COLUMN[7] + vz:, :] = jnp.zeros((640 - COLUMN[7] - vz, 256), F32)

    pl.semaphore_wait(barrier, NY + NZ - 2 + n_row - 1)
    for d in range(1, NY):
        e1_copy(d).start()
    phase_sums(0)
    start_far(0)
    start_own(0)
    start_far(1)
    phase_sums(1)
    e1[y] = e_ref[2 * y + core]
    for d in range(1, NY):
        e1_in(d).wait_recv()
    for yy in range(NY):
        ef[nv * yy:nv * yy + nv, :] = e1[yy].astype(F32)
    e2[z] = ef[...].astype(BF16)
    for d in range(1, NZ):
        e2_copy(d).start()
    start_sums(0)
    start_own(1)
    start_far(2)
    phase_sums(2)
    start_sums(1)
    start_own(2)
    start_far(3)
    phase_sums(3)
    rotations()
    start_sums(2)
    start_own(3)
    start_far(4)
    for d in range(1, NZ):
        e2_in(d).wait_recv()
    e3_copy().start()
    eigenvectors(e2, core)
    start_sums(3)
    start_own(4)
    start_far(5)
    e3_copy().wait_recv()
    eigenvectors(e3, 1 - core)
    branch(0)
    branch(1)
    start_sums(4)
    start_own(5)
    start_far(6)
    z_middle(0)
    branch(2)
    z_middle(1)
    branch(3)
    z_end(0)
    start_sums(5)
    start_own(6)
    start_far(7)
    z_end(1)
    z_middle(2)
    z_middle(3)
    branch(4)
    z_end(2)
    z_end(3)
    right_rotate(0)
    start_sums(6)
    start_own(7)
    z_middle(4)
    branch(5)
    z_end(4)
    start_sums(7)
    z_middle(5)
    branch(6)
    z_end(5)
    right_rotate(1)
    z_middle(6)
    branch(7)
    z_end(6)
    right_rotate(2)
    z_middle(7)
    row_wait(0)
    row_wait(1)
    z_end(7)
    right_rotate(3)
    row_wait(2)
    left_rotate(range(7), True)
    row_wait(3)
    left_rotate((7,), False)

    def o_copy(d):
        return remote(osend.at[lax.rem(y + d, NY)], out_ref.at[y], o_s.at[d], o_r.at[y], lat=ypeer(d))

    def o_in(d):
        yy = lax.rem(y + d, NY)
        return remote(osend.at[yy], out_ref.at[yy], o_s.at[d], o_r.at[yy], lat=ypeer(d))

    size = 4 * nv
    for yy in range(NY):
        osend[yy] = jnp.concatenate(
            [jnp.concatenate([ob[k, t, size * yy:size * yy + size, :] for t in range(2)], axis=1) for k in (0, 1)],
            axis=0).astype(BF16)
    for d in range(1, NY):
        o_copy(d).start()
    out_ref[y] = osend[y]

    for d in range(1, NY):
        e1_copy(d).wait_send()
    for d in range(1, NZ):
        e2_copy(d).wait_send()
    e3_copy().wait_send()
    for u in range(UNITS):
        for way in (0, 1):
            far(u, way).wait_send()
            for half in (0, 1):
                near(u, way, half).wait_send()
        z_copy_a(u).wait_send()
        z_copy_b(u).wait_send()
    for w in range(len(WINDOWS)):
        @pl.loop(1, n_row)
        def _(p):
            row_copy(w, p).wait_send()
    for d in range(1, NY):
        o_in(d).wait_recv()
        o_copy(d).wait_send()


def phases(qgrid, lattice, degeneracy):
    product = jnp.sum(qgrid[:, None, :] * lattice[None, :, :], axis=-1) % FINE
    angle = 2.0 * math.pi / FINE * product.astype(F32)
    weight = 1.0 / degeneracy.astype(F32)
    return jnp.cos(angle) * weight[None, :], jnp.sin(angle) * weight[None, :]


def per_device(n_row, g_wannier, lattice, degeneracy, qgrid, phonon_vectors, wannier_k, wannier_kq):
    n_r, modes, rows_m, wide = g_wannier.shape
    width = wide // 2
    points, nv, _ = phonon_vectors.shape
    full = -(-modes // 16) * 16
    vz = NY * nv

    cosines, sines = phases(qgrid, lattice, degeneracy)
    phase = jnp.concatenate([cosines, sines], axis=1).astype(BF16)
    phase = jnp.pad(phase, ((0, 16 - points), (0, 128 - 2 * n_r)))
    g = jnp.transpose(g_wannier, (2, 0, 1, 3))
    tail = jnp.pad(g[:, :, full - 16:], ((0, 0), (0, 0), (0, full - modes), (0, 0)))

    dma = pltpu.SemaphoreType.DMA
    vmem = pl.BlockSpec(memory_space=pltpu.VMEM)
    widths = [hi - lo for lo, hi in WINDOWS]
    out = pl.pallas_call(
        functools.partial(kernel, n_row),
        out_shape=jax.ShapeDtypeStruct((NY, 8 * nv, wide), BF16),
        in_specs=[vmem] * 6,
        out_specs=vmem,
        scratch_shapes=[
            pltpu.VMEM((points, rows_m, full, wide), BF16),
            pltpu.VMEM((UNITS, full, wide), BF16),
            pltpu.VMEM((UNITS, 2, full, wide), BF16),
            pltpu.VMEM((NY, nv, 2 * modes), BF16),
            pltpu.VMEM((NZ, vz, 2 * modes), BF16),
            pltpu.VMEM((NZ, vz, 2 * modes), BF16),
            pltpu.VMEM((vz, 2 * modes), F32),
            pltpu.VMEM((2, NZ * vz, 2 * full), BF16),
            pltpu.VMEM((UNITS, 2, 2, vz, wide), BF16),
            pltpu.VMEM((UNITS, 2, vz, wide), BF16),
            pltpu.VMEM((UNITS, vz, wide), BF16),
            pltpu.VMEM((UNITS, vz, wide), BF16),
            pltpu.VMEM((WINDOWS[-1][1], wide), F32),
            pltpu.VMEM((wide, wide), BF16),
            pltpu.VMEM((2, 2, width, width), F32),
            pltpu.VMEM((UNITS, 2 * n_row, wide), BF16),
            *[pltpu.VMEM((n_row, wide // n_row, w), BF16) for w in widths],
            *[pltpu.VMEM((n_row, wide // n_row, w), BF16) for w in widths],
            pltpu.VMEM((WINDOWS[-1][1] // 128, wide, 128), F32),
            pltpu.VMEM((2, 2, 4 * vz, width), F32),
            pltpu.VMEM((NY, 8 * nv, wide), BF16),
            dma((UNITS, 2)), dma((UNITS, 2)),
            dma((UNITS, 2, 2)), dma((UNITS, 2, 2)),
            dma((NY + NZ + 1,)), dma((NY + NZ + 1,)),
            dma((UNITS,)), dma((UNITS,)), dma((UNITS,)), dma((UNITS,)),
            dma((len(WINDOWS), n_row)), dma((len(WINDOWS), n_row)),
            dma((NY,)), dma((NY,)),
        ],
        compiler_params=pltpu.CompilerParams(
            collective_id=0, has_side_effects=True, vmem_limit_bytes=36 * 1024 * 1024),
        name="interpolate",
    )(g, tail, phase, phonon_vectors, wannier_k, wannier_kq)
    out = out.reshape(NY, 2, nv, 4, wide).transpose(2, 0, 1, 3, 4)
    return out.reshape(nv, points, 4, wide).astype(F32)


def solution(mesh):
    in_specs = (
        P("lat", None, "row", None),
        P("lat", None),
        P("lat"),
        P(),
        P(None, "lat", None),
        P(),
        P(),
    )
    out_specs = P("lat", None, "row", None)
    return jax.shard_map(
        functools.partial(per_device, mesh.shape["row"]),
        mesh=mesh, in_specs=in_specs, out_specs=out_specs, check_vma=False)
```

```python
import functools
import math

import jax
import jax.numpy as jnp
from jax import lax
from jax.experimental import pallas as pl
from jax.experimental.pallas import tpu as pltpu
from jax.sharding import PartitionSpec as P

FINE = 40
NY = 4
NZ = 4
NH = 4
MESH = pl.DeviceIdType.MESH
F32 = jnp.float32
BF16 = jnp.bfloat16


def dot(a, b, contract=((1,), (0,))):
    return lax.dot_general(a, b, (contract, ((), ())), preferred_element_type=F32)


def times_i(x):
    half = x.shape[-1] // 2
    return jnp.concatenate([-x[:, half:], x[:, :half]], axis=1)


def iota(shape, dim):
    return lax.broadcasted_iota(jnp.int32, shape, dim)


def one_hot(condition):
    return jnp.where(condition, 1.0, 0.0).astype(BF16)


UNITS = 8
COLUMN = (0, 72, 144, 216, 288, 360, 432, 512)
WINDOWS = ((0, 256), (256, 384), (384, 512), (512, 640))


def kernel(rows, g_ref, tail_ref, lattice_ref, degeneracy_ref, q_ref, e_ref, wk_ref, wkq_ref, out_ref,
           part, yfar, ynear, e0, e1, e2, e3, ef, eb, spart, zin, sfull, rt, lf, lb,
           kt0, kt1, kt2, kt3, km0, km1, km2, km3, kr0, kr1, kr2, kr3, zf, ob, osend,
           y_s, yf_r, yn_r, e_s, e_r, z_s, z_r, near_z, r1_s, r1_r, r2_s, r2_r, o_s, o_r):
    n_row = rows
    kt, km, kr = (kt0, kt1, kt2, kt3), (km0, km1, km2, km3), (kr0, kr1, kr2, kr3)
    lat = lax.axis_index("lat")
    row = lax.axis_index("row")
    y = lax.rem(lat, NY)
    z = lax.div(lat, NY)
    core = lax.rem(row, 2)
    n_xc = n_row // NH
    zh, xc = lax.div(row, n_xc), lax.rem(row, n_xc)
    n_r, modes = g_ref.shape[1], g_ref.shape[2]
    full = part.shape[2]
    nv = e_ref.shape[0]
    vz = NY * nv

    def ypeer(d):
        return z * NY + lax.rem(y + d, NY)

    def zpeer(d):
        return lax.rem(z + d, NZ) * NY + y

    def zh_peer(d):
        return lax.rem(row + n_xc * d, n_row)

    def xc_peer(p):
        return zh * n_xc + lax.rem(xc + p, n_xc)

    def remote(src, dst, ss, rs, **dev):
        return pltpu.make_async_remote_copy(
            src_ref=src, dst_ref=dst, send_sem=ss, recv_sem=rs, device_id=dev, device_id_type=MESH)

    barrier = pltpu.get_barrier_semaphore()
    for d in range(1, NY):
        pl.semaphore_signal(barrier, inc=1, device_id={"lat": ypeer(d)}, device_id_type=MESH)
    for d in range(1, NZ):
        pl.semaphore_signal(barrier, inc=1, device_id={"lat": zpeer(d)}, device_id_type=MESH)

    for d in (1, NH - 1):
        pl.semaphore_signal(barrier, inc=1, device_id={"row": zh_peer(d)}, device_id_type=MESH)

    @pl.loop(1, n_xc)
    def _(p):
        pl.semaphore_signal(barrier, inc=1, device_id={"row": xc_peer(p)}, device_id_type=MESH)

    at_q, at_r = iota((16, 128), 0), iota((16, 128), 1)
    is_cos = at_r < n_r
    at_r = jnp.where(is_cos, at_r, at_r - n_r)
    product = jnp.zeros((16, 128), jnp.int32)
    weight = jnp.ones((16, 128), jnp.int32)
    for r in range(n_r):
        column = jnp.zeros((16, 128), jnp.int32)
        for q in range(8):
            whole = sum(q_ref[c, q] * lattice_ref[c, r] for c in range(3))
            column = jnp.where(at_q == q, lax.rem(lax.rem(whole, FINE) + FINE, FINE), column)
        product = jnp.where(at_r == r, column, product)
        weight = jnp.where(at_r == r, degeneracy_ref[r], weight)
    angle = 2.0 * math.pi / FINE * product.astype(F32)
    phase = jnp.where(is_cos, jnp.cos(angle), jnp.sin(angle)) / weight.astype(F32)
    phase = jnp.where((at_r < n_r) & (at_q < 8), phase, 0.0).astype(BF16)

    spread_rows = one_hot((iota((128, 16), 0) >> 4) == iota((128, 16), 1))
    spread_cols = one_hot(iota((128, 32 * n_r), 0) == (iota((128, 32 * n_r), 1) >> 4))
    same = (iota((128, 32 * n_r), 0) & 15) == (iota((128, 32 * n_r), 1) & 15)
    a = jnp.where(same, dot(dot(spread_rows, phase).astype(BF16), spread_cols), 0.0).astype(BF16)

    def phase_sums(m):
        for i in range(full // 16):
            if 16 * i + 16 <= modes:
                blocks = [g_ref[m, r, 16 * i:16 * i + 16, :] for r in range(n_r)]
            else:
                blocks = [tail_ref[m, r] for r in range(n_r)]
            stack = jnp.concatenate(blocks + [times_i(b) for b in blocks], axis=0)
            res = dot(a, stack).astype(BF16)
            for q in range(8):
                part[q, m, 16 * i:16 * i + 16, :] = res[16 * q:16 * q + 16, :]

    def e1_copy(d):
        yy = lax.rem(y + d, NY)
        return remote(e0.at[yy], e1.at[y], e_s.at[d], e_r.at[y], lat=ypeer(d))

    def e1_in(d):
        yy = lax.rem(y + d, NY)
        return remote(e0.at[yy], e1.at[yy], e_s.at[d], e_r.at[yy], lat=ypeer(d))

    def e2_copy(d):
        return remote(e2.at[z], e2.at[z], e_s.at[NY + d], e_r.at[NY + z], lat=zpeer(d))

    def e2_in(d):
        zz = lax.rem(z + d, NZ)
        return remote(e2.at[zz], e2.at[zz], e_s.at[NY + d], e_r.at[NY + zz], lat=zpeer(d))

    def e3_copy():
        return remote(e2, e3, e_s.at[NY + NZ], e_r.at[NY + NZ], row=row + 1 - 2 * core)

    def pick():
        rows_in, rows_out = 8 * nv, NY * nv
        at, to = iota((rows_out, rows_in), 0), iota((rows_out, rows_in), 1)
        wanted = to & 7
        chosen = jnp.zeros((rows_out, rows_in), jnp.bool_)
        for yy in range(NY):
            chosen = chosen | ((at - nv * yy == (to >> 3)) & (wanted == 2 * yy + core))
        both = e_ref[...].astype(F32).reshape(rows_in, 2 * modes).astype(BF16)
        res = dot(one_hot(chosen), both)
        for yy in range(NY):
            e0[yy] = res[nv * yy:nv * yy + nv].astype(BF16)

    def eigenvectors(source, k):
        whole = jnp.concatenate([source[zz].astype(F32) for zz in range(NZ)], axis=0).astype(BF16)
        at = iota((2 * modes, 2 * full), 0)
        to = iota((2 * modes, 2 * full), 1)
        spread = one_hot(jnp.where(at < modes, at, at + full - modes) == to)
        eb[k] = dot(whole, spread).astype(BF16)

    right, left = ypeer(1), ypeer(3)
    qa = 2 * lax.rem(y + 1, NY)
    qb = 2 * lax.rem(y + 2, NY)
    qc = 2 * lax.rem(y + 3, NY)

    def ways(u):
        cut = (full // 2 + 15) // 16 * 16
        cut = cut if u % 2 == 0 else full - cut
        return pl.ds(0, cut), pl.ds(cut, full - cut)

    def far(u, way):
        k, m = divmod(u, 4)
        here = ways(u)[way]
        return remote(part.at[qb + k, m, here], yfar.at[u, here], y_s.at[u], yf_r.at[u, way],
                      lat=(right, left)[way])

    def near(u, way, half):
        k, m = divmod(u, 4)
        here = ways(u)[half]
        q = (qa, qc)[way] + k
        return remote(part.at[q, m, here], ynear.at[u, way, here], y_s.at[u],
                      yn_r.at[u], lat=(right, left)[way])

    def start_far(u):
        for way in (0, 1):
            far(u, way).start()

    def start_own(u):
        for way in (0, 1):
            near(u, way, 1 - way).start()

    def start_sums(u):
        k, m = divmod(u, 4)
        for way in (0, 1):
            far(u, way).wait_recv()
            q = (qa, qc)[way] + k
            here = ways(u)[way]
            part[q, m, here, :] = (part[q, m, here, :].astype(F32) + yfar[u, here, :].astype(F32)).astype(BF16)
            near(u, way, way).start()

    def z_copy(u, d):
        return remote(spart.at[u, lax.rem(z + d, NZ)], zin.at[u, z], z_s, z_r.at[u], lat=zpeer(d))

    def z_all(u):
        return remote(spart.at[u, 0:NZ - 1], zin.at[u, 0:NZ - 1], z_s, z_r.at[u], lat=zpeer(1))

    def branch(u):
        k, m = divmod(u, 4)
        remote(part.at[0:2, m], ynear.at[u], y_s.at[u], yn_r.at[u], lat=right).wait_recv()
        total = (part[2 * y + k, m].astype(F32) + ynear[u, 0].astype(F32) + ynear[u, 1].astype(F32)).astype(BF16)
        res = dot(eb[k], jnp.concatenate([total, times_i(total)], axis=0))
        for zz in range(NZ):
            spart[u, zz] = res[vz * zz:vz * zz + vz].astype(BF16)
        for d in range(1, NZ):
            z_copy(u, d).start()

    def z_sum(u):
        z_all(u).wait_recv()
        total = spart[u, z].astype(F32)
        for d in range(1, NZ):
            total = total + zin[u, lax.rem(z + d, NZ)].astype(F32)
        sfull[COLUMN[u]:COLUMN[u] + vz, :] = total

    def step1(w, d):
        to = lax.rem(zh + d, NH)
        return remote(kt[w].at[to], km[w].at[zh], r1_s.at[w], r1_r.at[w], row=zh_peer(d))

    def step1_all(w):
        return remote(kt[w].at[0:NH - 1], km[w].at[0:NH - 1], r1_s.at[w], r1_r.at[w], row=zh_peer(1))

    def step2(w, p):
        return remote(km[w].at[:, lax.rem(xc + p, n_xc)], kr[w].at[:, xc], r2_s.at[w], r2_r.at[w], row=xc_peer(p))

    def step2_all(w):
        return remote(km[w].at[:, 0:n_xc - 1], kr[w].at[:, 0:n_xc - 1], r2_s.at[w], r2_r.at[w], row=xc_peer(1))

    def right_rotate(w):
        lo, hi = WINDOWS[w]
        res = dot(rt[...], sfull[lo:hi, :].astype(BF16), ((1,), (1,)))
        kt[w][...] = res.reshape(kt[w].shape).astype(BF16)
        for d in (2, 1, 3):
            step1(w, d).start()
        km[w][zh] = kt[w][zh]

    def row_forward(w):
        step1_all(w).wait_recv()

        @pl.loop(1, n_xc)
        def _(p):
            step2(w, p).start()

        for i in range(NH):
            kr[w][i, xc] = km[w][i, xc]

    def row_wait(w):
        step2_all(w).wait_recv()
        lo, hi = WINDOWS[w]
        got = kr[w][...].astype(F32).reshape(8 * n_row, hi - lo)
        for t in range((hi - lo) // 128):
            zf[lo // 128 + t] = got[:, 128 * t:128 * t + 128]

    def left_rotate(units, first):
        lo = COLUMN[units[0]] // 128
        hi = -(-(COLUMN[units[-1]] + vz) // 128)
        for n in range(4):
            w = jnp.concatenate(
                [jnp.concatenate([zf[t, pl.ds(n + 4 * c, n_row, stride=8), :] for c in (0, 1)], axis=0).T
                 for t in range(lo, hi)], axis=0)
            k = units[0] // 4
            acc = None
            for u in units:
                at = COLUMN[u] - 128 * lo
                term = dot(w[at:at + vz].astype(BF16), lb[u])
                acc = term if acc is None else acc + term
            for t in range(2):
                here = acc[:, 128 * t:128 * t + 128]
                if not first:
                    here = here + ob[k, t, pl.ds(n, vz, stride=4), :]
                ob[k, t, pl.ds(n, vz, stride=4), :] = here

    def o_copy(k, d):
        return remote(osend.at[k, lax.rem(y + d, NY)], out_ref.at[y, k], o_s.at[k, d], o_r.at[k, y], lat=ypeer(d))

    def o_in(k, d):
        yy = lax.rem(y + d, NY)
        return remote(osend.at[k, yy], out_ref.at[yy, k], o_s.at[k, d], o_r.at[k, yy], lat=ypeer(d))

    def send_result(k):
        size = 4 * nv
        for yy in range(NY):
            osend[k, yy] = jnp.concatenate(
                [ob[k, t, size * yy:size * yy + size, :] for t in range(2)], axis=1).astype(BF16)
        for d in (2, 1, 3):
            o_copy(k, d).start()
        out_ref[y, k] = osend[k, y]

    def rotations():
        r, j = iota((256, 256), 0), iota((256, 256), 1)
        perm = one_hot(j == ((r >> 2) & 1) * 128 + (r >> 3) * 4 + (r & 3))
        both = jnp.concatenate([wk_ref[...], times_i(wk_ref[...])], axis=0)
        rt[...] = dot(perm, both, ((1,), (1,))).astype(BF16)
        for k in (0, 1):
            for t in (0, 1):
                lf[k, t] = wkq_ref[2 * y + k, :, 128 * t:128 * t + 128].astype(F32)
        for u in range(UNITS):
            k, m = divmod(u, 4)
            ur = lf[k, 0, pl.ds(m, n_row, stride=4), :]
            ui = lf[k, 1, pl.ds(m, n_row, stride=4), :]
            lb[u] = jnp.concatenate([jnp.concatenate([ur, -ui], axis=1), jnp.concatenate([ui, ur], axis=1)],
                                    axis=0).astype(BF16)
        sfull[COLUMN[6] + vz:COLUMN[7], :] = jnp.zeros((COLUMN[7] - COLUMN[6] - vz, 256), F32)
        sfull[COLUMN[7] + vz:, :] = jnp.zeros((640 - COLUMN[7] - vz, 256), F32)

    pl.semaphore_wait(barrier, NY + NZ - 2 + 2 + n_xc - 1)
    pl.semaphore_signal(near_z, inc=1, device_id={"row": zh_peer(1)}, device_id_type=MESH)
    phase_sums(0)
    start_far(0)
    start_own(0)
    pick()
    for d in range(1, NY):
        e1_copy(d).start()
    e1[y] = e0[y]
    phase_sums(1)
    start_far(1)
    start_sums(0)
    start_own(1)
    phase_sums(2)
    start_far(2)
    for d in range(1, NY):
        e1_in(d).wait_recv()
    for yy in range(NY):
        ef[nv * yy:nv * yy + nv, :] = e1[yy].astype(F32)
    e2[z] = ef[...].astype(BF16)
    for d in range(1, NZ):
        e2_copy(d).start()
    start_sums(1)
    start_own(2)
    phase_sums(3)
    start_far(3)
    rotations()
    start_sums(2)
    start_own(3)
    start_far(4)
    for d in range(1, NZ):
        e2_in(d).wait_recv()
    e3_copy().start()
    eigenvectors(e2, core)
    start_sums(3)
    start_own(4)
    start_far(5)
    e3_copy().wait_recv()
    eigenvectors(e3, 1 - core)
    branch(0)
    branch(1)
    start_sums(4)
    start_own(5)
    start_far(6)
    branch(2)
    z_sum(0)
    branch(3)
    start_sums(5)
    start_own(6)
    start_far(7)
    z_sum(1)
    branch(4)
    z_sum(2)
    start_sums(6)
    start_own(7)
    z_sum(3)
    pl.semaphore_wait(near_z, 1)
    right_rotate(0)
    branch(5)
    start_sums(7)
    z_sum(4)
    branch(6)
    z_sum(5)
    right_rotate(1)
    branch(7)
    row_forward(0)
    z_sum(6)
    right_rotate(2)
    z_sum(7)
    right_rotate(3)
    row_forward(1)
    row_wait(0)
    row_forward(2)
    row_wait(1)
    left_rotate((0, 1, 2, 3), True)
    send_result(0)
    row_forward(3)
    row_wait(2)
    left_rotate((4, 5, 6), True)
    row_wait(3)
    left_rotate((7,), False)
    send_result(1)

    for d in range(1, NY):
        e1_copy(d).wait_send()
    for d in range(1, NZ):
        e2_copy(d).wait_send()
    e3_copy().wait_send()
    for u in range(UNITS):
        remote(part.at[0:3, 0], part.at[0:3, 0], y_s.at[u], yn_r.at[u], lat=right).wait_send()
    remote(spart.at[:, 0:NZ - 1], zin.at[:, 0:NZ - 1], z_s, z_r.at[0], lat=right).wait_send()
    for w in range(len(WINDOWS)):
        step1_all(w).wait_send()
        step2_all(w).wait_send()
    for k in (0, 1):
        for d in range(1, NY):
            o_in(k, d).wait_recv()
            o_copy(k, d).wait_send()


def per_device(n_row, g_wannier, lattice, degeneracy, qgrid, phonon_vectors, wannier_k, wannier_kq):
    n_r, modes, rows_m, wide = g_wannier.shape
    width = wide // 2
    points, nv, _ = phonon_vectors.shape
    full = -(-modes // 16) * 16
    vz = NY * nv

    g = jnp.transpose(g_wannier, (2, 0, 1, 3))
    tail = jnp.pad(g[:, :, full - 16:], ((0, 0), (0, 0), (0, full - modes), (0, 0)))

    phonon = jnp.transpose(phonon_vectors, (1, 0, 2))

    dma = pltpu.SemaphoreType.DMA
    vmem = pl.BlockSpec(memory_space=pltpu.VMEM)
    smem = pl.BlockSpec(memory_space=pltpu.SMEM)
    widths = [hi - lo for lo, hi in WINDOWS]
    out = pl.pallas_call(
        functools.partial(kernel, n_row),
        out_shape=jax.ShapeDtypeStruct((NY, 2, 4 * nv, wide), BF16),
        in_specs=[vmem, vmem, smem, smem, smem, vmem, vmem, vmem],
        out_specs=vmem,
        scratch_shapes=[
            pltpu.VMEM((points, rows_m, full, wide), BF16),
            pltpu.VMEM((UNITS, full, wide), BF16),
            pltpu.VMEM((UNITS, 2, full, wide), BF16),
            pltpu.VMEM((NY, nv, 2 * modes), BF16),
            pltpu.VMEM((NY, nv, 2 * modes), BF16),
            pltpu.VMEM((NZ, vz, 2 * modes), BF16),
            pltpu.VMEM((NZ, vz, 2 * modes), BF16),
            pltpu.VMEM((vz, 2 * modes), F32),
            pltpu.VMEM((2, NZ * vz, 2 * full), BF16),
            pltpu.VMEM((UNITS, NZ, vz, wide), BF16),
            pltpu.VMEM((UNITS, NZ, vz, wide), BF16),
            pltpu.VMEM((WINDOWS[-1][1], wide), F32),
            pltpu.VMEM((wide, wide), BF16),
            pltpu.VMEM((2, 2, width, width), F32),
            pltpu.VMEM((UNITS, 2 * n_row, wide), BF16),
            *[pltpu.VMEM((NH, n_row // NH, wide // n_row, w), BF16) for w in widths * 3],
            pltpu.VMEM((WINDOWS[-1][1] // 128, wide, 128), F32),
            pltpu.VMEM((2, 2, 4 * vz, width), F32),
            pltpu.VMEM((2, NY, 4 * nv, wide), BF16),
            dma((UNITS,)), dma((UNITS, 2)), dma((UNITS,)),
            dma((NY + NZ + 1,)), dma((NY + NZ + 1,)),
            dma, dma((UNITS,)), pltpu.SemaphoreType.REGULAR,
            *[dma((len(WINDOWS),))] * 4,
            dma((2, NY)), dma((2, NY)),
        ],
        compiler_params=pltpu.CompilerParams(
            collective_id=0, has_side_effects=True, vmem_limit_bytes=36 * 1024 * 1024),
        name="interpolate",
    )(g, tail, lattice.T, degeneracy, qgrid.T, phonon, wannier_k, wannier_kq)
    out = out.reshape(NY, 2, nv, 4, wide).transpose(2, 0, 1, 3, 4)
    return out.reshape(nv, points, 4, wide).astype(F32)


def solution(mesh):
    in_specs = (
        P("lat", None, "row", None),
        P("lat", None),
        P("lat"),
        P(),
        P(None, "lat", None),
        P(),
        P(),
    )
    out_specs = P("lat", None, "row", None)
    return jax.shard_map(
        functools.partial(per_device, mesh.shape["row"]),
        mesh=mesh, in_specs=in_specs, out_specs=out_specs, check_vma=False)
```

```python
import functools
import math

import jax
import jax.numpy as jnp
from jax import lax
from jax.experimental import pallas as pl
from jax.experimental.pallas import tpu as pltpu
from jax.sharding import PartitionSpec as P

FINE = 40
NY = 4
NZ = 4
NH = 4
NX = 4
MESH = pl.DeviceIdType.MESH
F32 = jnp.float32
BF16 = jnp.bfloat16


def dot(a, b, contract=((1,), (0,))):
    return lax.dot_general(a, b, (contract, ((), ())), preferred_element_type=F32)


def times_i(x):
    half = x.shape[-1] // 2
    return jnp.concatenate([-x[:, half:], x[:, :half]], axis=1)


def iota(shape, dim):
    return lax.broadcasted_iota(jnp.int32, shape, dim)


def one_hot(condition):
    return jnp.where(condition, 1.0, 0.0).astype(BF16)


UNITS = 8
COLUMN = (0, 72, 144, 216, 288, 360, 432, 512)
WINDOWS = ((0, 256), (256, 384), (384, 512), (512, 640))


def kernel(rows, g_ref, tail_ref, lattice_ref, degeneracy_ref, q_ref, e_ref, wk_ref, wkq_ref, out_ref,
           part, yfar, ynear, e0, e1, e2, e3, ef, eb, spart, zin, sfull, rt, lb,
           kt0, kt1, kt2, kt3, km0, km1, km2, km3, kr0, kr1, kr2, kr3, zf, ob, osend,
           y_s, yf_r, yn_r, e_s, e_r, z_s, z_r, near_z, near_c, r1_s, r1_r, r2_s, r2_r, o_s, o_r):
    n_row = rows
    kt, km, kr = (kt0, kt1, kt2, kt3), (km0, km1, km2, km3), (kr0, kr1, kr2, kr3)
    lat = lax.axis_index("lat")
    row = lax.axis_index("row")
    y = lax.rem(lat, NY)
    z = lax.div(lat, NY)
    core = lax.rem(row, 2)
    zh, x = lax.div(row, 2 * NX), lax.rem(lax.div(row, 2), NX)
    group, n_group = zh * 2 + core, 2 * NH
    n_r, modes = g_ref.shape[1], g_ref.shape[2]
    full = part.shape[2]
    nv = e_ref.shape[0]
    vz = NY * nv

    def ypeer(d):
        return z * NY + lax.rem(y + d, NY)

    def zpeer(d):
        return lax.rem(z + d, NZ) * NY + y

    def zh_peer(d):
        return lax.rem(row + 2 * NX * d, n_row)

    def x_peer(d):
        return zh * 2 * NX + lax.rem(x + d, NX) * 2 + core

    def group_peer(p):
        to = lax.rem(group + p, n_group)
        return lax.div(to, 2) * 2 * NX + x * 2 + lax.rem(to, 2)

    def remote(src, dst, ss, rs, **dev):
        return pltpu.make_async_remote_copy(
            src_ref=src, dst_ref=dst, send_sem=ss, recv_sem=rs, device_id=dev, device_id_type=MESH)

    barrier = pltpu.get_barrier_semaphore()
    for d in range(1, NY):
        pl.semaphore_signal(barrier, inc=1, device_id={"lat": ypeer(d)}, device_id_type=MESH)
    for d in range(1, NZ):
        pl.semaphore_signal(barrier, inc=1, device_id={"lat": zpeer(d)}, device_id_type=MESH)

    for d in (1, NH - 1):
        pl.semaphore_signal(barrier, inc=1, device_id={"row": zh_peer(d)}, device_id_type=MESH)

    for d in range(1, NX):
        pl.semaphore_signal(barrier, inc=1, device_id={"row": x_peer(d)}, device_id_type=MESH)
    pl.semaphore_signal(barrier, inc=1, device_id={"row": row + 1 - 2 * core}, device_id_type=MESH)

    at_q, at_r = iota((16, 128), 0), iota((16, 128), 1)
    is_cos = at_r < n_r
    at_r = jnp.where(is_cos, at_r, at_r - n_r)
    product = jnp.zeros((16, 128), jnp.int32)
    weight = jnp.ones((16, 128), jnp.int32)
    for r in range(n_r):
        column = jnp.zeros((16, 128), jnp.int32)
        for q in range(8):
            whole = sum(q_ref[c, q] * lattice_ref[c, r] for c in range(3))
            column = jnp.where(at_q == q, lax.rem(lax.rem(whole, FINE) + FINE, FINE), column)
        product = jnp.where(at_r == r, column, product)
        weight = jnp.where(at_r == r, degeneracy_ref[r], weight)
    angle = 2.0 * math.pi / FINE * product.astype(F32)
    phase = jnp.where(is_cos, jnp.cos(angle), jnp.sin(angle)) / weight.astype(F32)
    phase = jnp.where((at_r < n_r) & (at_q < 8), phase, 0.0).astype(BF16)

    spread_rows = one_hot((iota((128, 16), 0) >> 4) == iota((128, 16), 1))
    spread_cols = one_hot(iota((128, 32 * n_r), 0) == (iota((128, 32 * n_r), 1) >> 4))
    same = (iota((128, 32 * n_r), 0) & 15) == (iota((128, 32 * n_r), 1) & 15)
    a = jnp.where(same, dot(dot(spread_rows, phase).astype(BF16), spread_cols), 0.0).astype(BF16)

    def phase_sums(m):
        for i in range(full // 16):
            if 16 * i + 16 <= modes:
                blocks = [g_ref[m, r, 16 * i:16 * i + 16, :] for r in range(n_r)]
            else:
                blocks = [tail_ref[m, r] for r in range(n_r)]
            stack = jnp.concatenate(blocks + [times_i(b) for b in blocks], axis=0)
            res = dot(a, stack).astype(BF16)
            for q in range(8):
                part[q, m, 16 * i:16 * i + 16, :] = res[16 * q:16 * q + 16, :]

    def e1_copy(d):
        yy = lax.rem(y + d, NY)
        return remote(e0.at[yy], e1.at[y], e_s.at[d], e_r.at[y], lat=ypeer(d))

    def e1_in(d):
        yy = lax.rem(y + d, NY)
        return remote(e0.at[yy], e1.at[yy], e_s.at[d], e_r.at[yy], lat=ypeer(d))

    def e2_copy(d):
        return remote(e2.at[z], e2.at[z], e_s.at[NY + d], e_r.at[NY + z], lat=zpeer(d))

    def e2_in(d):
        zz = lax.rem(z + d, NZ)
        return remote(e2.at[zz], e2.at[zz], e_s.at[NY + d], e_r.at[NY + zz], lat=zpeer(d))

    def e3_copy():
        return remote(e2, e3, e_s.at[NY + NZ], e_r.at[NY + NZ], row=row + 1 - 2 * core)

    def pick():
        rows_in, rows_out = 8 * nv, NY * nv
        at, to = iota((rows_out, rows_in), 0), iota((rows_out, rows_in), 1)
        wanted = to & 7
        chosen = jnp.zeros((rows_out, rows_in), jnp.bool_)
        for yy in range(NY):
            chosen = chosen | ((at - nv * yy == (to >> 3)) & (wanted == 2 * yy + core))
        both = e_ref[...].astype(F32).reshape(rows_in, 2 * modes).astype(BF16)
        res = dot(one_hot(chosen), both)
        for yy in range(NY):
            e0[yy] = res[nv * yy:nv * yy + nv].astype(BF16)

    def eigenvectors(source, k):
        whole = jnp.concatenate([source[zz].astype(F32) for zz in range(NZ)], axis=0).astype(BF16)
        at = iota((2 * modes, 2 * full), 0)
        to = iota((2 * modes, 2 * full), 1)
        spread = one_hot(jnp.where(at < modes, at, at + full - modes) == to)
        eb[k] = dot(whole, spread).astype(BF16)

    right, left = ypeer(1), ypeer(3)
    qa = 2 * lax.rem(y + 1, NY)
    qb = 2 * lax.rem(y + 2, NY)
    qc = 2 * lax.rem(y + 3, NY)

    def ways(u):
        cut = (full // 2 + 15) // 16 * 16
        cut = cut if u % 2 == 0 else full - cut
        return pl.ds(0, cut), pl.ds(cut, full - cut)

    def far(u, way):
        k, m = divmod(u, 4)
        here = ways(u)[way]
        return remote(part.at[qb + k, m, here], yfar.at[u, here], y_s.at[u], yf_r.at[u, way],
                      lat=(right, left)[way])

    def near(u, way, half):
        k, m = divmod(u, 4)
        here = ways(u)[half]
        q = (qa, qc)[way] + k
        return remote(part.at[q, m, here], ynear.at[u, way, here], y_s.at[u],
                      yn_r.at[u], lat=(right, left)[way])

    def start_far(u):
        for way in (0, 1):
            far(u, way).start()

    def start_own(u):
        for way in (0, 1):
            near(u, way, 1 - way).start()

    def start_sums(u):
        k, m = divmod(u, 4)
        for way in (0, 1):
            far(u, way).wait_recv()
            q = (qa, qc)[way] + k
            here = ways(u)[way]
            part[q, m, here, :] = (part[q, m, here, :].astype(F32) + yfar[u, here, :].astype(F32)).astype(BF16)
            near(u, way, way).start()

    def z_copy(u, d):
        return remote(spart.at[u, lax.rem(z + d, NZ)], zin.at[u, z], z_s, z_r.at[u], lat=zpeer(d))

    def z_all(u):
        return remote(spart.at[u, 0:NZ - 1], zin.at[u, 0:NZ - 1], z_s, z_r.at[u], lat=zpeer(1))

    def branch(u):
        k, m = divmod(u, 4)
        remote(part.at[0:2, m], ynear.at[u], y_s.at[u], yn_r.at[u], lat=right).wait_recv()
        total = (part[2 * y + k, m].astype(F32) + ynear[u, 0].astype(F32) + ynear[u, 1].astype(F32)).astype(BF16)
        res = dot(eb[k], jnp.concatenate([total, times_i(total)], axis=0))
        for zz in range(NZ):
            spart[u, zz] = res[vz * zz:vz * zz + vz].astype(BF16)
        for d in range(1, NZ):
            z_copy(u, d).start()

    def z_sum(u):
        z_all(u).wait_recv()
        total = spart[u, z].astype(F32)
        for d in range(1, NZ):
            total = total + zin[u, lax.rem(z + d, NZ)].astype(F32)
        sfull[COLUMN[u]:COLUMN[u] + vz, :] = total

    def step1(w, p):
        to = lax.rem(group + p, n_group)
        return remote(kt[w].at[to], km[w].at[group], r1_s.at[w], r1_r.at[w], row=group_peer(p))

    def step1_all(w):
        return remote(kt[w].at[0:n_group - 1], km[w].at[0:n_group - 1], r1_s.at[w], r1_r.at[w], row=group_peer(1))

    def step2(w, d):
        return remote(km[w].at[:, lax.rem(x + d, NX)], kr[w].at[:, x], r2_s.at[w], r2_r.at[w], row=x_peer(d))

    def step2_all(w):
        return remote(km[w].at[:, 0:NX - 1], kr[w].at[:, 0:NX - 1], r2_s.at[w], r2_r.at[w], row=x_peer(1))

    def right_rotate(w):
        lo, hi = WINDOWS[w]
        res = dot(rt[...], sfull[lo:hi, :].astype(BF16), ((1,), (1,)))
        kt[w][...] = res.reshape(kt[w].shape).astype(BF16)
        for p in (4, 3, 5, 2, 6, 1, 7):
            step1(w, p).start()
        km[w][group] = kt[w][group]

    def row_forward(w):
        step1_all(w).wait_recv()
        for d in (2, 1, 3):
            step2(w, d).start()
        for i in range(n_group):
            kr[w][i, x] = km[w][i, x]

    def row_wait(w):
        step2_all(w).wait_recv()
        lo, hi = WINDOWS[w]
        got = kr[w][...].astype(F32).reshape(8 * n_row, hi - lo)
        for t in range((hi - lo) // 128):
            zf[lo // 128 + t] = got[:, 128 * t:128 * t + 128]

    def left_rotate(units, first):
        lo = COLUMN[units[0]] // 128
        hi = -(-(COLUMN[units[-1]] + vz) // 128)
        for n in range(4):
            w = jnp.concatenate(
                [jnp.concatenate([zf[t, pl.ds(n + 4 * c, n_row, stride=8), :] for c in (0, 1)], axis=0).T
                 for t in range(lo, hi)], axis=0)
            k = units[0] // 4
            acc = None
            for u in units:
                at = COLUMN[u] - 128 * lo
                term = dot(w[at:at + vz].astype(BF16), lb[u])
                acc = term if acc is None else acc + term
            for t in range(2):
                here = acc[:, 128 * t:128 * t + 128]
                if not first:
                    here = here + ob[k, t, pl.ds(n, vz, stride=4), :]
                ob[k, t, pl.ds(n, vz, stride=4), :] = here

    def o_copy(k, d):
        return remote(osend.at[k, lax.rem(y + d, NY)], out_ref.at[y, k], o_s.at[k, d], o_r.at[k, y], lat=ypeer(d))

    def o_in(k, d):
        yy = lax.rem(y + d, NY)
        return remote(osend.at[k, yy], out_ref.at[yy, k], o_s.at[k, d], o_r.at[k, yy], lat=ypeer(d))

    def send_result(k):
        size = 4 * nv
        for yy in range(NY):
            osend[k, yy] = jnp.concatenate(
                [ob[k, t, size * yy:size * yy + size, :] for t in range(2)], axis=1).astype(BF16)
        for d in (2, 1, 3):
            o_copy(k, d).start()
        out_ref[y, k] = osend[k, y]

    def rotations():
        r, j = iota((256, 256), 0), iota((256, 256), 1)
        block = (r >> 6) * 8 + ((r >> 3) & 3) * 2 + ((r >> 5) & 1)
        perm = one_hot(j == ((r >> 2) & 1) * 128 + block * 4 + (r & 3))
        both = jnp.concatenate([wk_ref[...], times_i(wk_ref[...])], axis=0)
        rt[...] = dot(perm, both, ((1,), (1,))).astype(BF16)
        r, j = iota((n_row, 128), 0), iota((n_row, 128), 1)
        block = (r >> 3) * 8 + (r & 3) * 2 + ((r >> 2) & 1)
        for u in range(UNITS):
            k, m = divmod(u, 4)
            left_rows = dot(one_hot(j == block * 4 + m), wkq_ref[2 * y + k])
            ur, ui = left_rows[:, :128], left_rows[:, 128:]
            lb[u] = jnp.concatenate([jnp.concatenate([ur, -ui], axis=1), jnp.concatenate([ui, ur], axis=1)],
                                    axis=0).astype(BF16)
        sfull[COLUMN[6] + vz:COLUMN[7], :] = jnp.zeros((COLUMN[7] - COLUMN[6] - vz, 256), F32)
        sfull[COLUMN[7] + vz:, :] = jnp.zeros((640 - COLUMN[7] - vz, 256), F32)

    phase_sums(0)
    pl.semaphore_wait(barrier, NY + NZ + NX)
    start_far(0)
    start_own(0)
    pl.semaphore_signal(near_z, inc=1, device_id={"row": zh_peer(1)}, device_id_type=MESH)
    pick()
    for d in (2, 1, 3):
        e1_copy(d).start()
    e1[y] = e0[y]
    phase_sums(1)
    start_far(1)
    phase_sums(2)
    start_far(2)
    start_sums(0)
    start_own(1)
    phase_sums(3)
    start_far(3)
    for d in range(1, NY):
        e1_in(d).wait_recv()
    for yy in range(NY):
        ef[nv * yy:nv * yy + nv, :] = e1[yy].astype(F32)
    e2[z] = ef[...].astype(BF16)
    for d in range(1, NZ):
        e2_copy(d).start()
    start_sums(1)
    start_own(2)
    start_far(4)
    rotations()
    start_sums(2)
    start_own(3)
    start_far(5)
    pl.semaphore_wait(near_z, 1)
    pl.semaphore_signal(near_c, inc=1, device_id={"row": row + 1 - 2 * core}, device_id_type=MESH)
    for d in range(1, NZ):
        e2_in(d).wait_recv()
    e3_copy().start()
    eigenvectors(e2, core)
    start_sums(3)
    start_own(4)
    start_far(6)
    e3_copy().wait_recv()
    eigenvectors(e3, 1 - core)
    branch(0)
    branch(1)
    start_sums(4)
    start_own(5)
    start_far(7)
    branch(2)
    z_sum(0)
    branch(3)
    start_sums(5)
    start_own(6)
    z_sum(1)
    branch(4)
    z_sum(2)
    start_sums(6)
    start_own(7)
    z_sum(3)
    pl.semaphore_wait(near_c, 1)
    right_rotate(0)
    branch(5)
    start_sums(7)
    z_sum(4)
    branch(6)
    z_sum(5)
    right_rotate(1)
    branch(7)
    row_forward(0)
    z_sum(6)
    right_rotate(2)
    z_sum(7)
    right_rotate(3)
    row_forward(1)
    row_wait(0)
    row_forward(2)
    row_wait(1)
    row_forward(3)
    left_rotate((0, 1, 2, 3), True)
    send_result(0)
    row_wait(2)
    left_rotate((4, 5, 6), True)
    row_wait(3)
    left_rotate((7,), False)
    send_result(1)

    for d in range(1, NY):
        e1_copy(d).wait_send()
    for d in range(1, NZ):
        e2_copy(d).wait_send()
    e3_copy().wait_send()
    for u in range(UNITS):
        remote(part.at[0:3, 0], part.at[0:3, 0], y_s.at[u], yn_r.at[u], lat=right).wait_send()
    remote(spart.at[:, 0:NZ - 1], zin.at[:, 0:NZ - 1], z_s, z_r.at[0], lat=right).wait_send()
    for w in range(len(WINDOWS)):
        step1_all(w).wait_send()
        step2_all(w).wait_send()
    for k in (0, 1):
        for d in range(1, NY):
            o_in(k, d).wait_recv()
            o_copy(k, d).wait_send()


def per_device(n_row, g_wannier, lattice, degeneracy, qgrid, phonon_vectors, wannier_k, wannier_kq):
    n_r, modes, rows_m, wide = g_wannier.shape
    width = wide // 2
    points, nv, _ = phonon_vectors.shape
    full = -(-modes // 16) * 16
    vz = NY * nv

    g = jnp.transpose(g_wannier, (2, 0, 1, 3))
    tail = jnp.pad(g[:, :, full - 16:], ((0, 0), (0, 0), (0, full - modes), (0, 0)))

    phonon = jnp.transpose(phonon_vectors, (1, 0, 2))

    dma = pltpu.SemaphoreType.DMA
    vmem = pl.BlockSpec(memory_space=pltpu.VMEM)
    smem = pl.BlockSpec(memory_space=pltpu.SMEM)
    widths = [hi - lo for lo, hi in WINDOWS]
    out = pl.pallas_call(
        functools.partial(kernel, n_row),
        out_shape=jax.ShapeDtypeStruct((NY, 2, 4 * nv, wide), BF16),
        in_specs=[vmem, vmem, smem, smem, smem, vmem, vmem, vmem],
        out_specs=vmem,
        scratch_shapes=[
            pltpu.VMEM((points, rows_m, full, wide), BF16),
            pltpu.VMEM((UNITS, full, wide), BF16),
            pltpu.VMEM((UNITS, 2, full, wide), BF16),
            pltpu.VMEM((NY, nv, 2 * modes), BF16),
            pltpu.VMEM((NY, nv, 2 * modes), BF16),
            pltpu.VMEM((NZ, vz, 2 * modes), BF16),
            pltpu.VMEM((NZ, vz, 2 * modes), BF16),
            pltpu.VMEM((vz, 2 * modes), F32),
            pltpu.VMEM((2, NZ * vz, 2 * full), BF16),
            pltpu.VMEM((UNITS, NZ, vz, wide), BF16),
            pltpu.VMEM((UNITS, NZ, vz, wide), BF16),
            pltpu.VMEM((WINDOWS[-1][1], wide), F32),
            pltpu.VMEM((wide, wide), BF16),
            pltpu.VMEM((UNITS, 2 * n_row, wide), BF16),
            *[pltpu.VMEM((2 * NH, NX, wide // n_row, w), BF16) for w in widths * 3],
            pltpu.VMEM((WINDOWS[-1][1] // 128, wide, 128), F32),
            pltpu.VMEM((2, 2, 4 * vz, width), F32),
            pltpu.VMEM((2, NY, 4 * nv, wide), BF16),
            dma((UNITS,)), dma((UNITS, 2)), dma((UNITS,)),
            dma((NY + NZ + 1,)), dma((NY + NZ + 1,)),
            dma, dma((UNITS,)), pltpu.SemaphoreType.REGULAR, pltpu.SemaphoreType.REGULAR,
            *[dma((len(WINDOWS),))] * 4,
            dma((2, NY)), dma((2, NY)),
        ],
        compiler_params=pltpu.CompilerParams(
            collective_id=0, has_side_effects=True, vmem_limit_bytes=36 * 1024 * 1024),
        name="interpolate",
    )(g, tail, lattice.T, degeneracy, qgrid.T, phonon, wannier_k, wannier_kq)
    out = out.reshape(NY, 2, nv, 4, wide).transpose(2, 0, 1, 3, 4)
    return out.reshape(nv, points, 4, wide).astype(F32)


def solution(mesh):
    in_specs = (
        P("lat", None, "row", None),
        P("lat", None),
        P("lat"),
        P(),
        P(None, "lat", None),
        P(),
        P(),
    )
    out_specs = P("lat", None, "row", None)
    return jax.shard_map(
        functools.partial(per_device, mesh.shape["row"]),
        mesh=mesh, in_specs=in_specs, out_specs=out_specs, check_vma=False)
```

```python
import functools
import math

import jax
import jax.numpy as jnp
from jax import lax
from jax.experimental import pallas as pl
from jax.experimental.pallas import tpu as pltpu
from jax.sharding import PartitionSpec as P

FINE = 40
NY = 4
NZ = 4
NH = 4
NX = 4
MESH = pl.DeviceIdType.MESH
F32 = jnp.float32
BF16 = jnp.bfloat16


def dot(a, b, contract=((1,), (0,))):
    return lax.dot_general(a, b, (contract, ((), ())), preferred_element_type=F32)


def times_i(x):
    half = x.shape[-1] // 2
    return jnp.concatenate([-x[:, half:], x[:, :half]], axis=1)


def iota(shape, dim):
    return lax.broadcasted_iota(jnp.int32, shape, dim)


def one_hot(condition):
    return jnp.where(condition, 1.0, 0.0).astype(BF16)


UNITS = 8
COLUMN = (0, 72, 144, 216, 288, 360, 432, 512)
WINDOWS = ((0, 256), (256, 384), (384, 512), (512, 640))
LAST = len(WINDOWS) - 1


def kernel(rows, g_ref, tail_ref, lattice_ref, degeneracy_ref, q_ref, e_ref, wk_ref, wkq_ref, out_ref,
           part, yfar, ynear, e0, e1, e2, e3, ef, eb, spart, zin, sfull, rt, lb,
           kt0, kt1, kt2, kt3, km0, km1, km2, kr0, kr1, kr2, kr3, zf, ob, osend,
           y_s, yf_r, yn_r, e_s, e_r, z_s, z_r, near_z, near_c, near_x, r1_s, r1_r, r2_s, r2_r, o_s, o_r):
    n_row = rows
    kt, km, kr = (kt0, kt1, kt2, kt3), (km0, km1, km2), (kr0, kr1, kr2, kr3)
    lat = lax.axis_index("lat")
    row = lax.axis_index("row")
    y = lax.rem(lat, NY)
    z = lax.div(lat, NY)
    core = lax.rem(row, 2)
    zh, x = lax.div(row, 2 * NX), lax.rem(lax.div(row, 2), NX)
    group, n_group = zh * 2 + core, 2 * NH
    n_r, modes = g_ref.shape[1], g_ref.shape[2]
    full = part.shape[2]
    nv = e_ref.shape[0]
    vz = NY * nv

    def ypeer(d):
        return z * NY + lax.rem(y + d, NY)

    def zpeer(d):
        return lax.rem(z + d, NZ) * NY + y

    def zh_peer(d):
        return lax.rem(row + 2 * NX * d, n_row)

    def x_peer(d):
        return zh * 2 * NX + lax.rem(x + d, NX) * 2 + core

    def group_peer(p):
        to = lax.rem(group + p, n_group)
        return lax.div(to, 2) * 2 * NX + x * 2 + lax.rem(to, 2)

    def remote(src, dst, ss, rs, **dev):
        return pltpu.make_async_remote_copy(
            src_ref=src, dst_ref=dst, send_sem=ss, recv_sem=rs, device_id=dev, device_id_type=MESH)

    barrier = pltpu.get_barrier_semaphore()
    for d in (1, NH - 1):
        pl.semaphore_signal(barrier, inc=1, device_id={"row": zh_peer(d)}, device_id_type=MESH)
    for d in range(1, NZ):
        pl.semaphore_signal(barrier, inc=1, device_id={"lat": zpeer(d)}, device_id_type=MESH)
    for d in (2, 1, 3):
        pl.semaphore_signal(barrier, inc=1, device_id={"lat": ypeer(d)}, device_id_type=MESH)
    for d in (2, 1, 3):
        pl.semaphore_signal(barrier, inc=1, device_id={"row": x_peer(d)}, device_id_type=MESH)
    pl.semaphore_signal(barrier, inc=1, device_id={"row": row + 1 - 2 * core}, device_id_type=MESH)

    at_q, at_r = iota((16, 128), 0), iota((16, 128), 1)
    is_cos = at_r < n_r
    at_r = jnp.where(is_cos, at_r, at_r - n_r)
    product = jnp.zeros((16, 128), jnp.int32)
    weight = jnp.ones((16, 128), jnp.int32)
    for r in range(n_r):
        column = jnp.zeros((16, 128), jnp.int32)
        for q in range(8):
            whole = sum(q_ref[c, q] * lattice_ref[c, r] for c in range(3))
            column = jnp.where(at_q == q, lax.rem(lax.rem(whole, FINE) + FINE, FINE), column)
        product = jnp.where(at_r == r, column, product)
        weight = jnp.where(at_r == r, degeneracy_ref[r], weight)
    angle = 2.0 * math.pi / FINE * product.astype(F32)
    phase = jnp.where(is_cos, jnp.cos(angle), jnp.sin(angle)) / weight.astype(F32)
    phase = jnp.where((at_r < n_r) & (at_q < 8), phase, 0.0).astype(BF16)

    spread_rows = one_hot((iota((128, 16), 0) >> 4) == iota((128, 16), 1))
    spread_cols = one_hot(iota((128, 32 * n_r), 0) == (iota((128, 32 * n_r), 1) >> 4))
    same = (iota((128, 32 * n_r), 0) & 15) == (iota((128, 32 * n_r), 1) & 15)
    a = jnp.where(same, dot(dot(spread_rows, phase).astype(BF16), spread_cols), 0.0).astype(BF16)

    def phase_sums(m):
        for i in range(full // 16):
            if 16 * i + 16 <= modes:
                blocks = [g_ref[m, r, 16 * i:16 * i + 16, :] for r in range(n_r)]
            else:
                blocks = [tail_ref[m, r] for r in range(n_r)]
            stack = jnp.concatenate(blocks + [times_i(b) for b in blocks], axis=0)
            res = dot(a, stack).astype(BF16)
            for q in range(8):
                part[q, m, 16 * i:16 * i + 16, :] = res[16 * q:16 * q + 16, :]

    def e1_copy(d):
        yy = lax.rem(y + d, NY)
        return remote(e0.at[yy], e1.at[y], e_s.at[d], e_r.at[y], lat=ypeer(d))

    def e1_in(d):
        yy = lax.rem(y + d, NY)
        return remote(e0.at[yy], e1.at[yy], e_s.at[d], e_r.at[yy], lat=ypeer(d))

    def e2_copy(d):
        return remote(e2.at[z], e2.at[z], e_s.at[NY + d], e_r.at[NY + z], lat=zpeer(d))

    def e2_in(d):
        zz = lax.rem(z + d, NZ)
        return remote(e2.at[zz], e2.at[zz], e_s.at[NY + d], e_r.at[NY + zz], lat=zpeer(d))

    def e3_copy():
        return remote(e2, e3, e_s.at[NY + NZ], e_r.at[NY + NZ], row=row + 1 - 2 * core)

    def pick():
        rows_in, rows_out = 8 * nv, NY * nv
        at, to = iota((rows_out, rows_in), 0), iota((rows_out, rows_in), 1)
        wanted = to & 7
        chosen = jnp.zeros((rows_out, rows_in), jnp.bool_)
        for yy in range(NY):
            chosen = chosen | ((at - nv * yy == (to >> 3)) & (wanted == 2 * yy + core))
        both = e_ref[...].astype(F32).reshape(rows_in, 2 * modes).astype(BF16)
        res = dot(one_hot(chosen), both)
        for yy in range(NY):
            e0[yy] = res[nv * yy:nv * yy + nv].astype(BF16)

    def eigenvectors(source, k):
        whole = jnp.concatenate([source[zz].astype(F32) for zz in range(NZ)], axis=0).astype(BF16)
        at = iota((2 * modes, 2 * full), 0)
        to = iota((2 * modes, 2 * full), 1)
        spread = one_hot(jnp.where(at < modes, at, at + full - modes) == to)
        eb[k] = dot(whole, spread).astype(BF16)

    right, left = ypeer(1), ypeer(3)
    qa = 2 * lax.rem(y + 1, NY)
    qb = 2 * lax.rem(y + 2, NY)
    qc = 2 * lax.rem(y + 3, NY)

    def ways(u):
        cut = (full // 2 + 15) // 16 * 16
        cut = cut if u % 2 == 0 else full - cut
        return pl.ds(0, cut), pl.ds(cut, full - cut)

    def far(u, way):
        k, m = divmod(u, 4)
        here = ways(u)[way]
        return remote(part.at[qb + k, m, here], yfar.at[u, here], y_s.at[u], yf_r.at[u, way],
                      lat=(right, left)[way])

    def near(u, way, half):
        k, m = divmod(u, 4)
        here = ways(u)[half]
        q = (qa, qc)[way] + k
        return remote(part.at[q, m, here], ynear.at[u, way, here], y_s.at[u],
                      yn_r.at[u], lat=(right, left)[way])

    def start_far(u):
        for way in (0, 1):
            far(u, way).start()

    def start_own(u):
        for way in (0, 1):
            near(u, way, 1 - way).start()

    def start_sums(u):
        k, m = divmod(u, 4)
        for way in (0, 1):
            far(u, way).wait_recv()
            q = (qa, qc)[way] + k
            here = ways(u)[way]
            part[q, m, here, :] = (part[q, m, here, :].astype(F32) + yfar[u, here, :].astype(F32)).astype(BF16)
            near(u, way, way).start()

    def z_copy(u, d):
        return remote(spart.at[u, lax.rem(z + d, NZ)], zin.at[u, z], z_s, z_r.at[u], lat=zpeer(d))

    def z_all(u):
        return remote(spart.at[u, 0:NZ - 1], zin.at[u, 0:NZ - 1], z_s, z_r.at[u], lat=zpeer(1))

    def branch(u):
        k, m = divmod(u, 4)
        remote(part.at[0:2, m], ynear.at[u], y_s.at[u], yn_r.at[u], lat=right).wait_recv()
        total = (part[2 * y + k, m].astype(F32) + ynear[u, 0].astype(F32) + ynear[u, 1].astype(F32)).astype(BF16)
        res = dot(eb[k], jnp.concatenate([total, times_i(total)], axis=0))
        for zz in range(NZ):
            spart[u, zz] = res[vz * zz:vz * zz + vz].astype(BF16)
        for d in range(1, NZ):
            z_copy(u, d).start()

    def z_sum(u):
        z_all(u).wait_recv()
        total = spart[u, z].astype(F32)
        for d in range(1, NZ):
            total = total + zin[u, lax.rem(z + d, NZ)].astype(F32)
        sfull[COLUMN[u]:COLUMN[u] + vz, :] = total

    def step1(w, p):
        to = lax.rem(group + p, n_group)
        return remote(kt[w].at[to], km[w].at[group], r1_s.at[w], r1_r.at[w], row=group_peer(p))

    def step1_all(w):
        return remote(kt[w].at[0:n_group - 1], km[w].at[0:n_group - 1], r1_s.at[w], r1_r.at[w], row=group_peer(1))

    def step2(w, d):
        return remote(km[w].at[:, lax.rem(x + d, NX)], kr[w].at[:, x], r2_s.at[w], r2_r.at[w], row=x_peer(d))

    def step2_all(w):
        return remote(km[w].at[:, 0:NX - 1], kr[w].at[:, 0:NX - 1], r2_s.at[w], r2_r.at[w], row=x_peer(1))

    def right_rotate(w):
        lo, hi = WINDOWS[w]
        res = dot(rt[...], sfull[lo:hi, :].astype(BF16), ((1,), (1,)))
        kt[w][...] = res.reshape(kt[w].shape).astype(BF16)
        if w < LAST:
            for p in (4, 3, 5, 2, 6, 1, 7):
                step1(w, p).start()
            km[w][group] = kt[w][group]

    def straight(p):
        to = lax.rem(row + p, n_row)
        at = (lax.div(to, 2 * NX) * 2 + lax.rem(to, 2)) * NX + lax.rem(lax.div(to, 2), NX)
        return remote(kt[LAST].at[at], kr[LAST].at[group * NX + x], r2_s.at[LAST], r2_r.at[LAST], row=to)

    def straight_all():
        return remote(kt[LAST].at[0:n_row - 1], kr[LAST].at[0:n_row - 1], r2_s.at[LAST], r2_r.at[LAST],
                      row=x_peer(1))

    def start_straight(lo, hi):
        @pl.loop(lo, hi)
        def _(p):
            straight(p).start()


    def row_forward(w):
        step1_all(w).wait_recv()
        for d in (2, 1, 3):
            step2(w, d).start()
        for i in range(n_group):
            kr[w][i, x] = km[w][i, x]

    def row_wait(w):
        (step2_all(w) if w < LAST else straight_all()).wait_recv()
        lo, hi = WINDOWS[w]
        got = kr[w][...].astype(F32).reshape(8 * n_row, hi - lo)
        for t in range((hi - lo) // 128):
            zf[lo // 128 + t] = got[:, 128 * t:128 * t + 128]

    def left_rotate(units, first):
        lo = COLUMN[units[0]] // 128
        hi = -(-(COLUMN[units[-1]] + vz) // 128)
        for n in range(4):
            w = jnp.concatenate(
                [jnp.concatenate([zf[t, pl.ds(n + 4 * c, n_row, stride=8), :] for c in (0, 1)], axis=0).T
                 for t in range(lo, hi)], axis=0)
            k = units[0] // 4
            acc = None
            for u in units:
                at = COLUMN[u] - 128 * lo
                term = dot(w[at:at + vz].astype(BF16), lb[u])
                acc = term if acc is None else acc + term
            for t in range(2):
                here = acc[:, 128 * t:128 * t + 128]
                if not first:
                    here = here + ob[k, t, pl.ds(n, vz, stride=4), :]
                ob[k, t, pl.ds(n, vz, stride=4), :] = here

    def o_copy(k, d):
        return remote(osend.at[k, lax.rem(y + d, NY)], out_ref.at[y, k], o_s.at[k, d], o_r.at[k, y], lat=ypeer(d))

    def o_in(k, d):
        yy = lax.rem(y + d, NY)
        return remote(osend.at[k, yy], out_ref.at[yy, k], o_s.at[k, d], o_r.at[k, yy], lat=ypeer(d))

    def send_result(k):
        size = 4 * nv
        for yy in range(NY):
            osend[k, yy] = jnp.concatenate(
                [ob[k, t, size * yy:size * yy + size, :] for t in range(2)], axis=1).astype(BF16)
        for d in (2, 1, 3):
            o_copy(k, d).start()
        out_ref[y, k] = osend[k, y]

    def rotations():
        r, j = iota((256, 256), 0), iota((256, 256), 1)
        block = (r >> 6) * 8 + ((r >> 3) & 3) * 2 + ((r >> 5) & 1)
        perm = one_hot(j == ((r >> 2) & 1) * 128 + block * 4 + (r & 3))
        both = jnp.concatenate([wk_ref[...], times_i(wk_ref[...])], axis=0)
        rt[...] = dot(perm, both, ((1,), (1,))).astype(BF16)
        r, j = iota((n_row, 128), 0), iota((n_row, 128), 1)
        block = (r >> 3) * 8 + (r & 3) * 2 + ((r >> 2) & 1)
        for u in range(UNITS):
            k, m = divmod(u, 4)
            left_rows = dot(one_hot(j == block * 4 + m), wkq_ref[2 * y + k])
            ur, ui = left_rows[:, :128], left_rows[:, 128:]
            lb[u] = jnp.concatenate([jnp.concatenate([ur, -ui], axis=1), jnp.concatenate([ui, ur], axis=1)],
                                    axis=0).astype(BF16)
        sfull[COLUMN[6] + vz:COLUMN[7], :] = jnp.zeros((COLUMN[7] - COLUMN[6] - vz, 256), F32)
        sfull[COLUMN[7] + vz:, :] = jnp.zeros((640 - COLUMN[7] - vz, 256), F32)

    phase_sums(0)
    pl.semaphore_wait(barrier, NY + NZ + NX)
    start_far(0)
    start_own(0)
    pl.semaphore_signal(near_z, inc=1, device_id={"row": zh_peer(1)}, device_id_type=MESH)
    pick()
    for d in (2, 1, 3):
        e1_copy(d).start()
    e1[y] = e0[y]
    phase_sums(1)
    start_far(1)
    phase_sums(2)
    start_far(2)
    start_sums(0)
    start_own(1)
    phase_sums(3)
    start_far(3)
    for d in range(1, NY):
        e1_in(d).wait_recv()
    for yy in range(NY):
        ef[nv * yy:nv * yy + nv, :] = e1[yy].astype(F32)
    e2[z] = ef[...].astype(BF16)
    for d in range(1, NZ):
        e2_copy(d).start()
    start_sums(1)
    start_own(2)
    start_far(4)
    rotations()
    start_sums(2)
    start_own(3)
    start_far(5)
    pl.semaphore_wait(near_z, 1)
    pl.semaphore_signal(near_c, inc=1, device_id={"row": row + 1 - 2 * core}, device_id_type=MESH)
    for d in range(1, NZ):
        e2_in(d).wait_recv()
    e3_copy().start()
    eigenvectors(e2, core)
    start_sums(3)
    start_own(4)
    start_far(6)
    e3_copy().wait_recv()
    eigenvectors(e3, 1 - core)
    branch(0)
    branch(1)
    start_sums(4)
    start_own(5)
    start_far(7)
    branch(2)
    z_sum(0)
    branch(3)
    start_sums(5)
    start_own(6)
    z_sum(1)
    branch(4)
    z_sum(2)
    start_sums(6)
    start_own(7)
    z_sum(3)
    pl.semaphore_wait(near_c, 1)
    for d in (2, 1, 3):
        pl.semaphore_signal(near_x, inc=1, device_id={"row": x_peer(d)}, device_id_type=MESH)
    right_rotate(0)
    branch(5)
    start_sums(7)
    z_sum(4)
    branch(6)
    z_sum(5)
    right_rotate(1)
    branch(7)
    row_forward(0)
    z_sum(6)
    right_rotate(2)
    z_sum(7)
    right_rotate(3)
    pl.semaphore_wait(near_x, NX - 1)
    start_straight(12, n_row)
    row_forward(1)
    start_straight(1, 12)
    kr[LAST][group * NX + x] = kt[LAST][group * NX + x]
    row_wait(0)
    row_forward(2)
    row_wait(1)
    left_rotate((0, 1, 2, 3), True)
    send_result(0)
    row_wait(2)
    left_rotate((4, 5, 6), True)
    row_wait(3)
    left_rotate((7,), False)
    send_result(1)

    for d in range(1, NY):
        e1_copy(d).wait_send()
    for d in range(1, NZ):
        e2_copy(d).wait_send()
    e3_copy().wait_send()
    for u in range(UNITS):
        remote(part.at[0:3, 0], part.at[0:3, 0], y_s.at[u], yn_r.at[u], lat=right).wait_send()
    remote(spart.at[:, 0:NZ - 1], zin.at[:, 0:NZ - 1], z_s, z_r.at[0], lat=right).wait_send()
    for w in range(LAST):
        step1_all(w).wait_send()
        step2_all(w).wait_send()
    straight_all().wait_send()
    for k in (0, 1):
        for d in range(1, NY):
            o_in(k, d).wait_recv()
            o_copy(k, d).wait_send()


def per_device(n_row, g_wannier, lattice, degeneracy, qgrid, phonon_vectors, wannier_k, wannier_kq):
    n_r, modes, rows_m, wide = g_wannier.shape
    width = wide // 2
    points, nv, _ = phonon_vectors.shape
    full = -(-modes // 16) * 16
    vz = NY * nv

    g = jnp.transpose(g_wannier, (2, 0, 1, 3))
    tail = jnp.pad(g[:, :, full - 16:], ((0, 0), (0, 0), (0, full - modes), (0, 0)))

    phonon = jnp.transpose(phonon_vectors, (1, 0, 2))

    dma = pltpu.SemaphoreType.DMA
    vmem = pl.BlockSpec(memory_space=pltpu.VMEM)
    smem = pl.BlockSpec(memory_space=pltpu.SMEM)
    widths = [hi - lo for lo, hi in WINDOWS]
    out = pl.pallas_call(
        functools.partial(kernel, n_row),
        out_shape=jax.ShapeDtypeStruct((NY, 2, 4 * nv, wide), BF16),
        in_specs=[vmem, vmem, smem, smem, smem, vmem, vmem, vmem],
        out_specs=vmem,
        scratch_shapes=[
            pltpu.VMEM((points, rows_m, full, wide), BF16),
            pltpu.VMEM((UNITS, full, wide), BF16),
            pltpu.VMEM((UNITS, 2, full, wide), BF16),
            pltpu.VMEM((NY, nv, 2 * modes), BF16),
            pltpu.VMEM((NY, nv, 2 * modes), BF16),
            pltpu.VMEM((NZ, vz, 2 * modes), BF16),
            pltpu.VMEM((NZ, vz, 2 * modes), BF16),
            pltpu.VMEM((vz, 2 * modes), F32),
            pltpu.VMEM((2, NZ * vz, 2 * full), BF16),
            pltpu.VMEM((UNITS, NZ, vz, wide), BF16),
            pltpu.VMEM((UNITS, NZ, vz, wide), BF16),
            pltpu.VMEM((WINDOWS[-1][1], wide), F32),
            pltpu.VMEM((wide, wide), BF16),
            pltpu.VMEM((UNITS, 2 * n_row, wide), BF16),
            *[pltpu.VMEM((2 * NH, NX, wide // n_row, w), BF16) for w in widths[:-1]],
            pltpu.VMEM((n_row, wide // n_row, widths[-1]), BF16),
            *[pltpu.VMEM((2 * NH, NX, wide // n_row, w), BF16) for w in widths[:-1] * 2],
            pltpu.VMEM((n_row, wide // n_row, widths[-1]), BF16),
            pltpu.VMEM((WINDOWS[-1][1] // 128, wide, 128), F32),
            pltpu.VMEM((2, 2, 4 * vz, width), F32),
            pltpu.VMEM((2, NY, 4 * nv, wide), BF16),
            dma((UNITS,)), dma((UNITS, 2)), dma((UNITS,)),
            dma((NY + NZ + 1,)), dma((NY + NZ + 1,)),
            dma, dma((UNITS,)), *[pltpu.SemaphoreType.REGULAR] * 3,
            *[dma((len(WINDOWS),))] * 4,
            dma((2, NY)), dma((2, NY)),
        ],
        compiler_params=pltpu.CompilerParams(
            collective_id=0, has_side_effects=True, vmem_limit_bytes=36 * 1024 * 1024),
        name="interpolate",
    )(g, tail, lattice.T, degeneracy, qgrid.T, phonon, wannier_k, wannier_kq)
    out = out.reshape(NY, 2, nv, 4, wide).transpose(2, 0, 1, 3, 4)
    return out.reshape(nv, points, 4, wide).astype(F32)


def solution(mesh):
    in_specs = (
        P("lat", None, "row", None),
        P("lat", None),
        P("lat"),
        P(),
        P(None, "lat", None),
        P(),
        P(),
    )
    out_specs = P("lat", None, "row", None)
    return jax.shard_map(
        functools.partial(per_device, mesh.shape["row"]),
        mesh=mesh, in_specs=in_specs, out_specs=out_specs, check_vma=False)
```
